32 devices in a mesh: tm: 8 (over y, x, core), space: 4 (over z).
Axes of the slice: x: 2, y: 2, z: 4, core: 2. Of those that a mesh axis runs over, the one named last changes fastest.
Arguments:
- snapshots: bfloat16 [4096, 8192], P('tm', 'space'), may hold values from -6 to 6
- outlier_cols: int32 [32, 16], P('tm', 'space'), may hold values from 0 to 15
- outlier_values: bfloat16 [32, 16, 128, 128], P('tm', 'space'), may hold values from -12 to 12
- threshold: float32 [], replicated, may hold values from 0.3 to 0.9
Outputs:
- gram_band: float32 [4096, 5, 512], P('tm', None, 'space')
The draws below stay inside these ranges and needn't reach their ends.
Inputs may be any that keep to these rules, and one draw needn't show every extreme that they name: `outlier_cols`: entry k of a row lies in the points of space block k // 4; repeated entries add.
All inputs are finite; a program needn't handle non-finite values.
Results may differ from the reference program's by a relative error of at most 0.0021.
Values may be sent and summed in bfloat16 or wider, within the bound.
No kernel may reach another device: no remote copies, remote signals or barrier semaphores. Data moves between devices by JAX's collectives and lax.ppermute only.
A program may use at most 128 MiB of HBM per device.

```python
import jax
import jax.numpy as jnp
from jax import lax

TB = 512
SP_DEV = 2048
OT = 128
ST = 128
KT = 4
TIME = 4096
SPACE = 8192
NH = 5
N_TM = 8
N_SPACE = 4


def plant(entries, own_key, least, high):
    longest = entries.shape.index(max(entries.shape))
    spots = []
    for shift in (0, 1):
        where = [jax.random.randint(jax.random.fold_in(own_key, axis), (), 0, length) for axis, length in enumerate(entries.shape)]
        where[longest] = (where[longest] + shift) % entries.shape[longest]
        spots.append(tuple(where))
    return entries.at[spots[0]].set(least).at[spots[1]].set(high)


def block_levels(own_key, shape, split, smallest, largest):
    def one(position, parts):
        draws = jax.random.uniform(jax.random.fold_in(jax.random.fold_in(own_key, 6), position), (parts,), jnp.float32, smallest / len(split), largest / len(split))
        return jnp.repeat(jnp.exp(draws), shape[position] // parts).reshape((-1,) + (1,) * (len(shape) - position - 1))

    loudness = one(*split[0])
    for cut in split[1:]:
        loudness = loudness * one(*cut)
    return loudness


def noise(stream_key, shape, deviation, most, split=(), held_as=jnp.bfloat16):
    values = jax.random.normal(stream_key, shape, jnp.float32) * deviation
    if len(split) > 0:
        values = block_levels(stream_key, shape, split, -0.22, 0.18) * values
    return jnp.clip(values, min=-most, max=most).astype(held_as)


def setup_inputs(seed: int = 0) -> dict:
    key_list = jax.random.split(jax.random.key(seed), 5)
    snapshots = noise(key_list[0], (TIME, SPACE), 1.0, 6.0, ((0, 8), (1, 4)))
    outlier_cols = plant(jax.random.randint(key_list[1], (TIME // OT, N_SPACE * KT), 0, SP_DEV // ST), jax.random.fold_in(key_list[1], 1), 0, (SP_DEV // ST) - 1).astype(jnp.int32)
    outlier_values = noise(key_list[2], (TIME // OT, N_SPACE * KT, OT, ST), 3.0, 12.0, ((0, 8), (1, 4)))
    threshold = jnp.clip(jax.random.uniform(key_list[3], (), jnp.float32, 0.3, 0.9), 0.3, 0.9)
    return {"snapshots": snapshots, "outlier_cols": outlier_cols, "outlier_values": outlier_values, "threshold": threshold}


def reference(snapshots, outlier_cols, outlier_values, threshold):
    rows = TIME // OT
    tiles_dev = SP_DEV // ST
    cols = outlier_cols.reshape(rows, N_SPACE, KT) + (jnp.arange(N_SPACE, dtype=jnp.int32) * tiles_dev)[None, :, None]
    cols = cols.reshape(rows, N_SPACE * KT)
    onehot = (cols[:, :, None] == jnp.arange(SPACE // ST, dtype=jnp.int32)[None, None, :]).astype(jnp.float32)

    def clean_rows(items):
        snap_rows, hot, vals = items
        dense = jnp.einsum('kos,kn->ons', vals.astype(jnp.float32), hot).reshape(OT, SPACE)
        diff = snap_rows.astype(jnp.float32) - dense
        return (jnp.sign(diff) * jnp.maximum(jnp.abs(diff) - threshold, 0.0)).astype(jnp.bfloat16)
    cleaned = lax.map(clean_rows, (snapshots.reshape(rows, OT, SPACE), onehot, outlier_values))
    blocks = cleaned.reshape(N_TM, TB, SPACE)
    scale = 1.0 / jnp.sqrt(jnp.float32(SPACE))

    def band_row(index):
        own = lax.dynamic_index_in_dim(blocks, index, 0, keepdims=False)
        tiles = []
        for step in range(NH):
            other = lax.dynamic_index_in_dim(blocks, (index + step) % N_TM, 0, keepdims=False)
            tiles.append(lax.dot_general(own, other, (((1,), (1,)), ((), ())), preferred_element_type=jnp.float32))
        return jnp.stack(tiles, axis=1) * scale
    band = lax.map(band_row, jnp.arange(N_TM, dtype=jnp.int32))
    return band.reshape(TIME, NH, TB)
```

```python
import math

import jax
import jax.numpy as jnp
from jax import lax
from jax.sharding import PartitionSpec as P

ST = 128
SNAP_MAX = 6.0
OUTLIER_MAX = 12.0
PARTS = 2


def swapped(x, axis, bit, only=None):
    pairs = [(i, i ^ bit) for i in range(lax.axis_size(axis)) if only is None or i & only]
    return lax.ppermute(x, axis, pairs)


def passed_along(x, axis, by):
    size = lax.axis_size(axis)
    return lax.ppermute(x, axis, [(i, (i + by) % size) for i in range(size)])


def tile_product(own, other):
    return lax.dot_general(own, other, (((1,), (1,)), ((), ())), preferred_element_type=jnp.float32)


def clean(snapshots, outlier_cols, outlier_values, threshold):
    block_rows, points = snapshots.shape
    tiles_dev = points // ST
    onehot = (
        outlier_cols[:, :, None] == jnp.arange(tiles_dev, dtype=jnp.int32)[None, None, :]
    ).astype(jnp.bfloat16)
    dense = jnp.einsum("rkos,rkn->rons", outlier_values, onehot, preferred_element_type=jnp.float32)
    dense = dense.reshape(block_rows, points)
    diff = snapshots.astype(jnp.float32) - dense
    return (jnp.sign(diff) * jnp.maximum(jnp.abs(diff) - threshold, 0.0)).astype(jnp.bfloat16)


def ring(cleaned):
    kept = [tile_product(cleaned, cleaned)]
    moving = cleaned
    for step in range(lax.axis_size("tm") // 2):
        moving = passed_along(moving, "tm", -1)
        kept.append(tile_product(cleaned, moving))
    return lax.psum_scatter(jnp.stack(kept, axis=1), "space", scatter_dimension=2, tiled=True)


def square(cleaned, most):
    rows, points = cleaned.shape
    quarter = rows // 4
    width = quarter // PARTS
    here = lax.axis_index("space")
    me = lax.axis_index("tm")
    core = me % 2
    far = (me // 2) % 2
    down = 2.0 ** -max(0, math.ceil(math.log2(2 * points * most * most / 6e4)))

    grouped = cleaned.reshape(4, quarter, points)
    own = [grouped[:, r * width : (r + 1) * width].reshape(4 * width, points) for r in range(PARTS)]

    def quarters(part, *which):
        part = part.reshape(4, width, points)
        return jnp.concatenate([lax.dynamic_index_in_dim(part, here ^ q, 0, keepdims=False) for q in which])

    def summed(blocks):
        away = [
            (tile_product(quarters(a, 1, 3), b) * down).astype(jnp.float16)
            for a, b in blocks
        ]
        away = swapped(jnp.stack(away).reshape(len(blocks), 2, width, 4 * width), "space", 1)
        stay = [tile_product(quarters(a, 0, 2), b) * down for a, b in blocks]
        stay = jnp.stack(stay).reshape(len(blocks), 2, width, 4 * width)
        stay = stay + away.astype(jnp.float32)
        away = swapped(stay[:, 1].astype(jnp.float16), "space", 2)
        return stay[:, 0] + away.astype(jnp.float32)

    by_x = [swapped(part, "tm", 2) for part in own]
    by_y = [swapped(part, "tm", 4) for part in own]
    sibling = [swapped(part, "tm", 1) for part in own]

    first = summed([(a, b) for a in own for b in own])
    first = {(r, s): first[r * PARTS + s] for r in range(PARTS) for s in range(PARTS)}
    tiles = {("own", r, s): v for (r, s), v in first.items()}

    left = []
    x_near, x_other = [], []
    for r in range(PARTS):
        x_near.append(by_x[r])
        x_other.append(swapped(by_x[r], "tm", 1))
        y_other = swapped(by_y[r], "tm", 1)
        side = jnp.where(core == 0, sibling[r], y_other)
        left.append(jnp.where(far == 1, by_y[r], own[r]))
        keys, blocks = [], []
        for s in range(PARTS):
            keys.append(("side", r, s))
            blocks.append((side, own[s]))
            keys.append(("y", r, s))
            blocks.append((by_y[r], own[s]))
        n_plain = len(keys)
        for s in range(r + 1):
            pairs = [(r, s)] if s == r else [(r, s), (s, r)]
            for i, j in pairs:
                keys.append(("near", i, j))
                blocks.append((x_near[i], left[j]))
                keys.append(("other", i, j))
                blocks.append((x_other[i], left[j]))
        done = summed(blocks)
        lent = swapped(done[n_plain:].astype(jnp.float16), "tm", 4, only=2).astype(jnp.float32)
        lent = jnp.where(far == 1, lent, done[n_plain:])
        for i, key in enumerate(keys):
            tiles[key] = done[i] if i < n_plain else lent[i - n_plain]

    def whole(name):
        tile = jnp.concatenate(
            [
                jnp.concatenate([tiles[name, r, s].reshape(width, 4, width) for s in range(PARTS)], axis=2)
                for r in range(PARTS)
            ],
            axis=0,
        )
        return tile.reshape(quarter, 4, quarter)

    one, three = whole("side"), whole("other")
    one, three = jnp.where(core == 0, one, three), jnp.where(core == 0, three, one)
    band = jnp.stack([whole("own"), one, whole("near"), three, whole("y")])
    band = band.reshape(5, quarter, rows).transpose(2, 0, 1)
    return band / down


def local(snapshots, outlier_cols, outlier_values, threshold):
    points = snapshots.shape[1]
    cleaned = clean(snapshots, outlier_cols, outlier_values, threshold)
    if lax.axis_size("tm") == 8 and lax.axis_size("space") == 4:
        band = square(cleaned, SNAP_MAX + outlier_cols.shape[1] * OUTLIER_MAX)
    else:
        band = ring(cleaned)
    return band * (1.0 / jnp.sqrt(jnp.float32(points * lax.axis_size("space"))))


def solution(mesh):
    placed = (P("tm", "space"), P("tm", "space"), P("tm", "space", None, None), P())
    return jax.shard_map(
        local, mesh=mesh, in_specs=placed, out_specs=P("tm", None, "space"), check_vma=False
    )
```

```python
import functools
import math

import jax
import jax.numpy as jnp
from jax import lax
from jax.experimental import pallas as pl
from jax.experimental.pallas import tpu as pltpu
from jax.sharding import PartitionSpec as P

ST = 128
SNAP_MAX = 6.0
OUTLIER_MAX = 12.0
UNITS = 4


def swapped(x, axis, bit, only=None):
    pairs = [(i, i ^ bit) for i in range(lax.axis_size(axis)) if only is None or only(i)]
    return lax.ppermute(x, axis, pairs)


def passed_along(x, axis, by):
    size = lax.axis_size(axis)
    return lax.ppermute(x, axis, [(i, (i + by) % size) for i in range(size)])


def tile_product(own, other):
    return lax.dot_general(own, other, (((1,), (1,)), ((), ())), preferred_element_type=jnp.float32)


def clean(snapshots, outlier_cols, outlier_values, threshold):
    block_rows, points = snapshots.shape
    tiles_dev = points // ST
    onehot = (
        outlier_cols[:, :, None] == jnp.arange(tiles_dev, dtype=jnp.int32)[None, None, :]
    ).astype(jnp.bfloat16)
    dense = jnp.einsum("rkos,rkn->rons", outlier_values, onehot, preferred_element_type=jnp.float32)
    dense = dense.reshape(block_rows, points)
    diff = snapshots.astype(jnp.float32) - dense
    return (jnp.sign(diff) * jnp.maximum(jnp.abs(diff) - threshold, 0.0)).astype(jnp.bfloat16)


def ring(cleaned):
    kept = [tile_product(cleaned, cleaned)]
    moving = cleaned
    for step in range(lax.axis_size("tm") // 2):
        moving = passed_along(moving, "tm", -1)
        kept.append(tile_product(cleaned, moving))
    return lax.psum_scatter(jnp.stack(kept, axis=1), "space", scatter_dimension=2, tiled=True)


def in_order(body, out_shape, n_in, n_after=0, scratch=()):
    anywhere = pl.BlockSpec(memory_space=pl.ANY)
    whole = pl.BlockSpec(memory_space=pltpu.VMEM)
    return pl.pallas_call(
        body,
        out_shape=out_shape,
        in_specs=[whole] * n_in + [anywhere] * n_after,
        out_specs=jax.tree.map(lambda _: whole, out_shape),
        scratch_shapes=scratch,
        compiler_params=pltpu.CompilerParams(vmem_limit_bytes=40 << 20),
        cost_estimate=pl.CostEstimate(flops=1000, bytes_accessed=1000, transcendentals=0),
    )


def clean_kernel(cols_ref, threshold_ref, snapshots_ref, values_ref, all_ref, *first_refs):
    row = pl.program_id(0)
    threshold = threshold_ref[0]
    listed = values_ref.shape[1]

    def shrunk(d):
        return (d - jnp.clip(d, -threshold, threshold)).astype(jnp.bfloat16)

    width = all_ref.shape[1]

    def put(unit, columns, value):
        all_ref[unit, :, columns] = value
        if unit < len(first_refs):
            first_refs[unit][:, columns] = value

    for unit in range(UNITS):
        rows = slice(unit * width, (unit + 1) * width)
        put(unit, slice(None), shrunk(snapshots_ref[rows, :].astype(jnp.float32)))
    for k in range(listed):
        col = cols_ref[row, k]
        columns = pl.ds(pl.multiple_of(col * ST, ST), ST)
        for unit in range(UNITS):
            rows = slice(unit * width, (unit + 1) * width)
            total = values_ref[0, k, rows, :].astype(jnp.float32)
            for other in range(listed):
                if other != k:
                    same = jnp.where(cols_ref[row, other] == col, 1.0, 0.0)
                    total = total + same * values_ref[0, other, rows, :].astype(jnp.float32)
            put(unit, columns, shrunk(snapshots_ref[rows, columns].astype(jnp.float32) - total))


def clean_units(snapshots, outlier_cols, outlier_values, threshold, first):
    rows, points = snapshots.shape
    tile_rows, listed, height, _ = outlier_values.shape
    width = height // UNITS
    unit = jax.ShapeDtypeStruct((rows // UNITS, points), jnp.bfloat16)
    return pl.pallas_call(
        clean_kernel,
        grid=(tile_rows,),
        out_shape=[jax.ShapeDtypeStruct((UNITS, rows // UNITS, points), jnp.bfloat16)] + [unit] * first,
        in_specs=[
            pl.BlockSpec(memory_space=pltpu.SMEM),
            pl.BlockSpec(memory_space=pltpu.SMEM),
            pl.BlockSpec((height, points), lambda g: (g, 0)),
            pl.BlockSpec((1, listed, height, ST), lambda g: (g, 0, 0, 0)),
        ],
        out_specs=[pl.BlockSpec((UNITS, width, points), lambda g: (0, g, 0))]
        + [pl.BlockSpec((width, points), lambda g: (g, 0))] * first,
        compiler_params=pltpu.CompilerParams(vmem_limit_bytes=40 << 20),
    )(outlier_cols, threshold.reshape(1), snapshots, outlier_values)


def columns_of(ref):
    here = lax.axis_index("space")
    width = ref.shape[0] // 4
    return jnp.concatenate(
        [ref[pl.ds(pl.multiple_of((here ^ q) * width, width), width), :] for q in (0, 2, 1, 3)], axis=0
    )


def multiply(cols, rows, down, stay_ref, away_ref, places):
    product = tile_product(jnp.concatenate(cols, axis=0), jnp.concatenate(rows, axis=0)) * down
    width, length = stay_ref.shape[2:]
    for c, line in enumerate(places):
        for s, place in enumerate(line):
            for q in range(4):
                top = (c * 4 + q) * width
                block = product[top : top + width, s * length : (s + 1) * length]
                (stay_ref, stay_ref, away_ref, away_ref)[q][q % 2, place] = block


def own_kernel(down, all_ref, stay_ref, away_ref):
    for c in range(UNITS):
        places = [[c * UNITS + s for s in range(UNITS)]]
        rows = [all_ref[s] for s in range(UNITS)]
        multiply([columns_of(all_ref.at[c])], rows, down, stay_ref, away_ref, places)


def x_blocks(unit):
    keys = [(name, unit, s) for name in ("near", "other") for s in range(unit + 1)]
    return keys + [(name, s, unit) for s in range(unit) for name in ("near", "other")]


def y_blocks(unit):
    return [(name, unit, s) for name in ("y", "side") for s in range(UNITS)]


def unit_kernel(down, unit, n_after, *refs):
    refs = list(refs)

    def take(n):
        out, refs[:n] = refs[:n], []
        return out

    all_ref, sibling_ref, y_ref, y_other_ref = take(4)
    near, other, left_before = take(unit + 1), take(unit + 1), take(unit)
    take(n_after)
    stay_ref, away_ref, left_ref = take(3)
    next_ref = take(1)[0] if unit + 2 < UNITS else None
    side_ref = refs[0]
    core = lax.rem(lax.axis_index("tm"), 2)
    far = lax.rem(lax.div(lax.axis_index("tm"), 2), 2)

    if next_ref is not None:
        next_ref[...] = all_ref[unit + 2]

    @pl.when(far == 1)
    def _():
        left_ref[...] = y_ref[...]

    @pl.when(far == 0)
    def _():
        left_ref[...] = all_ref[unit]

    @pl.when(core == 0)
    def _():
        side_ref[...] = sibling_ref[unit]

    @pl.when(core == 1)
    def _():
        side_ref[...] = y_other_ref[...]

    place = {key: i for i, key in enumerate(x_blocks(unit) + y_blocks(unit))}
    left = [ref[...] for ref in left_before] + [left_ref[...]]
    multiply(
        [columns_of(near[unit]), columns_of(other[unit])],
        left,
        down,
        stay_ref,
        away_ref,
        [[place[name, unit, s] for s in range(unit + 1)] for name in ("near", "other")],
    )
    if unit > 0:
        multiply(
            [columns_of(ref) for pair in zip(near[:unit], other[:unit]) for ref in pair],
            [left_ref[...]],
            down,
            stay_ref,
            away_ref,
            [[place[name, s, unit]] for s in range(unit) for name in ("near", "other")],
        )
    multiply(
        [columns_of(y_ref), columns_of(side_ref)],
        [all_ref[s] for s in range(UNITS)],
        down,
        stay_ref,
        away_ref,
        [[place[name, unit, s] for s in range(UNITS)] for name in ("y", "side")],
    )


def assemble_kernel(scale, *refs):
    own_ref, x_refs, y_refs, out_ref = refs[0], refs[1 : 1 + UNITS], refs[1 + UNITS : 1 + 2 * UNITS], refs[-1]
    core = lax.rem(lax.axis_index("tm"), 2)
    where = {("own", c, s): (own_ref, c * UNITS + s) for c in range(UNITS) for s in range(UNITS)}
    for unit in range(UNITS):
        where.update({key: (x_refs[unit], i) for i, key in enumerate(x_blocks(unit))})
        where.update({key: (y_refs[unit], i) for i, key in enumerate(y_blocks(unit))})
    width = own_ref.shape[1]
    quarter = width * UNITS

    def put(k, name):
        for s in range(UNITS):
            pieces = [where[name, c, s] for c in range(UNITS)]
            tile = jnp.concatenate([ref[i] for ref, i in pieces], axis=0).T * scale
            for g in range(4):
                out_ref[k, g * quarter + s * width : g * quarter + (s + 1) * width, :] = tile[g * width : (g + 1) * width]

    put(0, "own")
    put(2, "near")
    put(4, "y")

    @pl.when(core == 0)
    def _():
        put(1, "side")
        put(3, "other")

    @pl.when(core == 1)
    def _():
        put(1, "other")
        put(3, "side")


def square(snapshots, outlier_cols, outlier_values, threshold):
    rows, points = snapshots.shape
    width, length = rows // (4 * UNITS), rows // UNITS
    far = (lax.axis_index("tm") // 2) % 2
    most = SNAP_MAX + outlier_cols.shape[1] * OUTLIER_MAX
    down = 2.0 ** -max(0, math.ceil(math.log2(2 * points * most * most / 6e4)))
    scale = 1.0 / (math.sqrt(points * lax.axis_size("space")) * down)

    def message(blocks):
        return [jax.ShapeDtypeStruct((2, blocks, width, length), jnp.float32)] * 2

    def half_summed(stay, away):
        return stay + swapped(away.astype(jnp.float16), "space", 1).astype(jnp.float32)

    def summed(kept):
        return kept[0] + swapped(kept[1].astype(jnp.float16), "space", 2).astype(jnp.float32)

    whole, *sent = clean_units(snapshots, outlier_cols, outlier_values, threshold, 2)
    unit_shape = jax.ShapeDtypeStruct((length, points), jnp.bfloat16)
    sibling = swapped(whole, "tm", 1, lambda i: i % 2 == 1)
    near, other, by_y, left, halves, totals, x_parts, y_parts = [], [], [], [], [], [], [], []
    halves.append(half_summed(*in_order(functools.partial(own_kernel, down), message(UNITS * UNITS), 1)(whole)))
    for unit in range(UNITS):
        near.append(swapped(sent[unit], "tm", 2))
        by_y.append(swapped(sent[unit], "tm", 4))
        other.append(swapped(near[unit], "tm", 1))
        y_other = swapped(by_y[unit], "tm", 1, lambda i: i % 2 == 0)
        operands = [whole, sibling, by_y[unit], y_other, *near, *other, *left]
        after = [halves[-1]] + totals[-1:]
        more = unit + 2 < UNITS
        stay, away, now, *later = in_order(
            functools.partial(unit_kernel, down, unit, len(after)),
            message(len(x_blocks(unit)) + len(y_blocks(unit))) + [unit_shape] * (2 if more else 1),
            len(operands),
            len(after),
            [pltpu.VMEM((length, points), jnp.bfloat16)],
        )(*operands, *after)
        left.append(now)
        sent.extend(later)
        totals.append(summed(halves[-1]))
        halves.append(half_summed(stay, away))
    totals.append(summed(halves[-1]))
    for unit, total in enumerate(totals[1:]):
        n = len(x_blocks(unit))
        lent = swapped(total[:n].astype(jnp.float16), "tm", 4, lambda i: i & 2).astype(jnp.float32)
        x_parts.append(jnp.where(far == 1, lent, total[:n]))
        y_parts.append(total[n:])
    out_shape = jax.ShapeDtypeStruct((5, rows, rows // 4), jnp.float32)
    operands = [totals[0], *x_parts, *y_parts]
    band = in_order(functools.partial(assemble_kernel, scale), out_shape, len(operands))(*operands)
    return band.transpose(1, 0, 2)


def local(snapshots, outlier_cols, outlier_values, threshold):
    if lax.axis_size("tm") == 8 and lax.axis_size("space") == 4:
        return square(snapshots, outlier_cols, outlier_values, threshold)
    points = snapshots.shape[1] * lax.axis_size("space")
    band = ring(clean(snapshots, outlier_cols, outlier_values, threshold))
    return band * (1.0 / jnp.sqrt(jnp.float32(points)))


def solution(mesh):
    placed = (P("tm", "space"), P("tm", "space"), P("tm", "space", None, None), P())
    return jax.shard_map(
        local, mesh=mesh, in_specs=placed, out_specs=P("tm", None, "space"), check_vma=False
    )
```

```python
import functools
import math

import jax
import jax.numpy as jnp
from jax import lax
from jax.experimental import pallas as pl
from jax.experimental.pallas import tpu as pltpu
from jax.sharding import PartitionSpec as P

ST = 128
SNAP_MAX = 6.0
OUTLIER_MAX = 12.0
UNITS = 4
STAGES = ((0, 1), (2,), (3,))
GOES = ((0, 2), (2, 3))


def swapped(x, axis, bit, only=None):
    pairs = [(i, i ^ bit) for i in range(lax.axis_size(axis)) if only is None or only(i)]
    return lax.ppermute(x, axis, pairs)


def passed_along(x, axis, by):
    size = lax.axis_size(axis)
    return lax.ppermute(x, axis, [(i, (i + by) % size) for i in range(size)])


def tile_product(own, other):
    return lax.dot_general(own, other, (((1,), (1,)), ((), ())), preferred_element_type=jnp.float32)


def clean(snapshots, outlier_cols, outlier_values, threshold):
    block_rows, points = snapshots.shape
    tiles_dev = points // ST
    onehot = (
        outlier_cols[:, :, None] == jnp.arange(tiles_dev, dtype=jnp.int32)[None, None, :]
    ).astype(jnp.bfloat16)
    dense = jnp.einsum("rkos,rkn->rons", outlier_values, onehot, preferred_element_type=jnp.float32)
    dense = dense.reshape(block_rows, points)
    diff = snapshots.astype(jnp.float32) - dense
    return (jnp.sign(diff) * jnp.maximum(jnp.abs(diff) - threshold, 0.0)).astype(jnp.bfloat16)


def ring(cleaned):
    kept = [tile_product(cleaned, cleaned)]
    moving = cleaned
    for step in range(lax.axis_size("tm") // 2):
        moving = passed_along(moving, "tm", -1)
        kept.append(tile_product(cleaned, moving))
    return lax.psum_scatter(jnp.stack(kept, axis=1), "space", scatter_dimension=2, tiled=True)


def in_order(body, out_shape, n_in, n_after=0):
    anywhere = pl.BlockSpec(memory_space=pl.ANY)
    whole = pl.BlockSpec(memory_space=pltpu.VMEM)
    return pl.pallas_call(
        body,
        out_shape=out_shape,
        in_specs=[whole] * n_in + [anywhere] * n_after,
        out_specs=jax.tree.map(lambda _: whole, out_shape),
        compiler_params=pltpu.CompilerParams(vmem_limit_bytes=40 << 20),
        cost_estimate=pl.CostEstimate(flops=1000, bytes_accessed=1000, transcendentals=0),
    )


def clean_kernel(
    cols_hbm, threshold_ref, snapshots_hbm, values_hbm, all_ref, *refs
):
    *sent_refs, cols_ref, snapshots_ref, values_ref, cols_sem, row_sems, value_sems = refs
    tile_rows, listed, height, _ = values_ref.shape
    width = height // UNITS
    threshold = threshold_ref[0]
    cols_copy = pltpu.make_async_copy(cols_hbm, cols_ref, cols_sem)
    cols_copy.start()
    row_copies, value_copies = [], []
    for g in range(tile_rows):
        rows = pl.ds(g * height, height)
        row_copies.append(pltpu.make_async_copy(snapshots_hbm.at[rows], snapshots_ref.at[rows], row_sems.at[g]))
        value_copies.append(pltpu.make_async_copy(values_hbm.at[g], values_ref.at[g], value_sems.at[g]))
        row_copies[-1].start()
        value_copies[-1].start()
    cols_copy.wait()

    def shrunk(d):
        return (d - jnp.clip(d, -threshold, threshold)).astype(jnp.bfloat16)

    for g in range(tile_rows):
        row_copies[g].wait()

        def put(unit, columns, value):
            all_ref[unit, g * width : (g + 1) * width, columns] = value
            for stage, sent_ref in enumerate(sent_refs):
                if unit in STAGES[stage]:
                    top = (unit - STAGES[stage][0]) * height + g * width
                    sent_ref[top : top + width, columns] = value

        for unit in range(UNITS):
            rows = slice(g * height + unit * width, g * height + (unit + 1) * width)
            put(unit, slice(None), shrunk(snapshots_ref[rows, :].astype(jnp.float32)))
        value_copies[g].wait()
        for k in range(listed):
            col = cols_ref[g, k]
            columns = pl.ds(pl.multiple_of(col * ST, ST), ST)
            for unit in range(UNITS):
                rows = slice(unit * width, (unit + 1) * width)
                total = values_ref[g, k, rows, :].astype(jnp.float32)
                for other in range(listed):
                    if other != k:
                        same = jnp.where(cols_ref[g, other] == col, 1.0, 0.0)
                        total = total + same * values_ref[g, other, rows, :].astype(jnp.float32)
                rows = slice(g * height + unit * width, g * height + (unit + 1) * width)
                put(unit, columns, shrunk(snapshots_ref[rows, columns].astype(jnp.float32) - total))


def clean_units(snapshots, outlier_cols, outlier_values, threshold, first):
    rows, points = snapshots.shape
    tile_rows = outlier_values.shape[0]
    length = rows // UNITS
    out_shape = [jax.ShapeDtypeStruct((UNITS, length, points), jnp.bfloat16)]
    out_shape += [jax.ShapeDtypeStruct((len(units) * length, points), jnp.bfloat16) for units in STAGES[:first]]
    hbm = pl.BlockSpec(memory_space=pltpu.HBM)
    return pl.pallas_call(
        clean_kernel,
        out_shape=out_shape,
        in_specs=[hbm, pl.BlockSpec(memory_space=pltpu.SMEM), hbm, hbm],
        out_specs=[pl.BlockSpec(memory_space=pltpu.VMEM)] * len(out_shape),
        scratch_shapes=[
            pltpu.SMEM(outlier_cols.shape, jnp.int32),
            pltpu.VMEM(snapshots.shape, jnp.bfloat16),
            pltpu.VMEM(outlier_values.shape, jnp.bfloat16),
            pltpu.SemaphoreType.DMA,
            pltpu.SemaphoreType.DMA((tile_rows,)),
            pltpu.SemaphoreType.DMA((tile_rows,)),
        ],
        compiler_params=pltpu.CompilerParams(vmem_limit_bytes=40 << 20),
    )(outlier_cols, threshold.reshape(1), snapshots, outlier_values)


def columns_of(ref):
    here = lax.axis_index("space")
    width = ref.shape[0] // 4
    return [ref[pl.ds(pl.multiple_of((here ^ q) * width, width), width), :] for q in (0, 2, 1, 3)]


def multiply(cols, rows, down, stay_ref, away_ref, places):
    cols = [piece for ref in cols for piece in columns_of(ref)]
    product = tile_product(jnp.concatenate(cols, axis=0), jnp.concatenate([ref[...] for ref in rows], axis=0)) * down
    width, length = stay_ref.shape[2:]
    for c, line in enumerate(places):
        for s, place in enumerate(line):
            for q in range(4):
                top = (c * 4 + q) * width
                block = product[top : top + width, s * length : (s + 1) * length]
                (stay_ref, stay_ref, away_ref, away_ref)[q][q % 2, place] = block


def own_kernel(down, all_ref, stay_ref, away_ref, copy_ref):
    units = [all_ref.at[s] for s in range(UNITS)]
    for c in range(UNITS):
        multiply([units[c]], units, down, stay_ref, away_ref, [[c * UNITS + s for s in range(UNITS)]])
    copy_ref[...] = all_ref[...]


def x_blocks(stage):
    fresh, before = STAGES[stage], range(STAGES[stage][0])
    return [(c, s) for c in fresh for s in [*before, *fresh]] + [(c, s) for c in before for s in fresh]


def y_blocks(stage):
    return [(c, s) for c in STAGES[stage] for s in range(UNITS)]


def stage_blocks(stage):
    names = [("near", key) for key in x_blocks(stage)] + [("cross", key) for key in x_blocks(stage)]
    return names + [("y", key) for key in y_blocks(stage)] + [("side", key) for key in y_blocks(stage)]


def stage_kernel(down, stage, n_after, hands_on, *refs):
    refs = list(refs)

    def take(n):
        out, refs[:n] = refs[:n], []
        return out

    all_ref, sibling_ref, y_ref, y_other_ref = take(4)
    x_refs = take(stage + 1)
    left_before, cross_before = take(stage), take(stage)
    take(n_after)
    stay_ref, away_ref, left_ref, cross_ref, side_ref = take(5)
    core = lax.rem(lax.axis_index("tm"), 2)
    far = lax.rem(lax.div(lax.axis_index("tm"), 2), 2)
    fresh, before = STAGES[stage], STAGES[stage][0]
    first, count = fresh[0], len(fresh)
    length = all_ref.shape[1]

    def unit_of(ref, i):
        return ref.at[pl.ds(i * length, length)]

    def units_of(stage_refs):
        return [unit_of(ref, i) for s, ref in enumerate(stage_refs) for i in range(len(STAGES[s]))]

    if hands_on is not None:
        for i, unit in enumerate(STAGES[hands_on]):
            refs[0][i * length : (i + 1) * length] = all_ref[unit]

    for i, unit in enumerate(fresh):
        rows = slice(i * length, (i + 1) * length)

        @pl.when(far == 1)
        def _():
            left_ref[rows] = y_ref[rows]
            cross_ref[rows] = y_other_ref[rows]

        @pl.when(far == 0)
        def _():
            left_ref[rows] = all_ref[unit]
            cross_ref[rows] = sibling_ref[unit]

        @pl.when(core == 0)
        def _():
            side_ref[rows] = sibling_ref[unit]

        @pl.when(core == 1)
        def _():
            side_ref[rows] = y_other_ref[rows]

    place = {key: i for i, key in enumerate(stage_blocks(stage))}
    x_units = units_of(x_refs)
    left, cross = units_of([*left_before, left_ref]), units_of([*cross_before, cross_ref])
    n = first + count
    multiply(
        x_units[first:],
        left + cross,
        down,
        stay_ref,
        away_ref,
        [[place[name, (c, s)] for name in ("near", "cross") for s in range(n)] for c in fresh],
    )
    if before > 0:
        multiply(
            x_units[:first],
            left[first:] + cross[first:],
            down,
            stay_ref,
            away_ref,
            [[place[name, (c, s)] for name in ("near", "cross") for s in fresh] for c in range(before)],
        )
    multiply(
        [unit_of(ref, i) for ref in (y_ref, side_ref) for i in range(count)],
        [all_ref.at[s] for s in range(UNITS)],
        down,
        stay_ref,
        away_ref,
        [[place[name, (c, s)] for s in range(UNITS)] for name in ("y", "side") for c in fresh],
    )


def assemble_kernel(scale, *refs):
    own_ref, out_ref = refs[0], refs[-1]
    core = lax.rem(lax.axis_index("tm"), 2)
    where = {("own", (c, s)): (own_ref, c * UNITS + s) for c in range(UNITS) for s in range(UNITS)}
    rest = iter(refs[1:-1])
    for first, last in GOES:
        for name in ("near", "cross"):
            keys = [key for stage in range(first, last) for key in x_blocks(stage)]
            ref = next(rest)
            where.update({(name, key): (ref, i) for i, key in enumerate(keys)})
    for stage in range(len(STAGES)):
        ref = next(rest)
        keys = [(name, key) for name in ("y", "side") for key in y_blocks(stage)]
        where.update({key: (ref, i) for i, key in enumerate(keys)})
    width = own_ref.shape[1]
    quarter = width * UNITS

    def put(k, name):
        for s in range(UNITS):
            pieces = [where[name, (c, s)] for c in range(UNITS)]
            tile = jnp.concatenate([ref[i] for ref, i in pieces], axis=0).T * scale
            for g in range(4):
                out_ref[k, g * quarter + s * width : g * quarter + (s + 1) * width, :] = tile[g * width : (g + 1) * width]

    put(0, "own")
    put(2, "near")
    put(4, "y")

    @pl.when(core == 0)
    def _():
        put(1, "side")
        put(3, "cross")

    @pl.when(core == 1)
    def _():
        put(1, "cross")
        put(3, "side")


def square(snapshots, outlier_cols, outlier_values, threshold):
    rows, points = snapshots.shape
    width, length = rows // (4 * UNITS), rows // UNITS
    far = (lax.axis_index("tm") // 2) % 2
    most = SNAP_MAX + outlier_cols.shape[1] * OUTLIER_MAX
    down = 2.0 ** -max(0, math.ceil(math.log2(2 * points * most * most / 6e4)))
    scale = 1.0 / (math.sqrt(points * lax.axis_size("space")) * down)

    def message(blocks):
        return [jax.ShapeDtypeStruct((2, blocks, width, length), jnp.float32)] * 2

    def units(n):
        return jax.ShapeDtypeStruct((n * length, points), jnp.bfloat16)

    def half_summed(stay, away):
        return stay + swapped(away.astype(jnp.float16), "space", 1).astype(jnp.float32)

    def summed(kept):
        return kept[0] + swapped(kept[1].astype(jnp.float16), "space", 2).astype(jnp.float32)

    whole, *sent = clean_units(snapshots, outlier_cols, outlier_values, threshold, 2)
    out_shape = message(UNITS * UNITS) + [jax.ShapeDtypeStruct(whole.shape, whole.dtype)]
    stay, away, lent = in_order(functools.partial(own_kernel, down), out_shape, 1)(whole)
    sibling = swapped(lent, "tm", 1)
    own = summed(half_summed(stay, away))
    x_units, left, cross, totals = [], [], [], []
    for stage, fresh in enumerate(STAGES):
        x_units.append(swapped(sent[stage], "tm", 2))
        y_units = swapped(sent[stage], "tm", 4)
        y_other = swapped(y_units, "tm", 1)
        operands = [whole, sibling, y_units, y_other, *x_units, *left, *cross]
        after = ([], [own], totals[:1])[stage]
        hands_on = stage + 2 if stage + 2 < len(STAGES) else None
        out_shape = message(len(stage_blocks(stage))) + [units(len(fresh))] * 3
        if hands_on is not None:
            out_shape.append(units(len(STAGES[hands_on])))
        stay, away, left_now, cross_now, _, *later = in_order(
            functools.partial(stage_kernel, down, stage, len(after), hands_on), out_shape, len(operands), len(after)
        )(*operands, *after)
        left.append(left_now)
        cross.append(cross_now)
        sent.extend(later)
        totals.append(summed(half_summed(stay, away)))

    parts = []
    for first, last in GOES:
        near, other = [], []
        for stage in range(first, last):
            n = len(x_blocks(stage))
            near.append(totals[stage][:n])
            other.append(totals[stage][n : 2 * n])
        near, other = jnp.concatenate(near), jnp.concatenate(other)
        handed = swapped(near.astype(jnp.float16), "tm", 4, lambda i: i & 2)
        parts.append(jnp.where(far == 1, handed.astype(jnp.float32), near))
        pairs = [(i, i ^ (5 if i & 2 else 1)) for i in range(lax.axis_size("tm"))]
        parts.append(lax.ppermute(other.astype(jnp.float16), "tm", pairs).astype(jnp.float32))
    parts += [total[2 * len(x_blocks(stage)) :] for stage, total in enumerate(totals)]
    out_shape = jax.ShapeDtypeStruct((5, rows, rows // 4), jnp.float32)
    operands = [own, *parts]
    band = in_order(functools.partial(assemble_kernel, scale), out_shape, len(operands))(*operands)
    return band.transpose(1, 0, 2)


def local(snapshots, outlier_cols, outlier_values, threshold):
    if lax.axis_size("tm") == 8 and lax.axis_size("space") == 4:
        return square(snapshots, outlier_cols, outlier_values, threshold)
    points = snapshots.shape[1] * lax.axis_size("space")
    band = ring(clean(snapshots, outlier_cols, outlier_values, threshold))
    return band * (1.0 / jnp.sqrt(jnp.float32(points)))


def solution(mesh):
    placed = (P("tm", "space"), P("tm", "space"), P("tm", "space", None, None), P())
    return jax.shard_map(
        local, mesh=mesh, in_specs=placed, out_specs=P("tm", None, "space"), check_vma=False
    )
```

```python
import functools
import math

import jax
import jax.numpy as jnp
from jax import lax
from jax.experimental import pallas as pl
from jax.experimental.pallas import tpu as pltpu
from jax.sharding import PartitionSpec as P

ST = 128
SNAP_MAX = 6.0
OUTLIER_MAX = 12.0
UNITS = 4
STAGES = ((0, 1), (2,), (3,))
GOES = ((0, 2), (2, 3))


def swapped(x, axis, bit, only=None):
    pairs = [(i, i ^ bit) for i in range(lax.axis_size(axis)) if only is None or only(i)]
    return lax.ppermute(x, axis, pairs)


def passed_along(x, axis, by):
    size = lax.axis_size(axis)
    return lax.ppermute(x, axis, [(i, (i + by) % size) for i in range(size)])


def tile_product(own, other):
    return lax.dot_general(own, other, (((1,), (1,)), ((), ())), preferred_element_type=jnp.float32)


def clean(snapshots, outlier_cols, outlier_values, threshold):
    block_rows, points = snapshots.shape
    tiles_dev = points // ST
    onehot = (
        outlier_cols[:, :, None] == jnp.arange(tiles_dev, dtype=jnp.int32)[None, None, :]
    ).astype(jnp.bfloat16)
    dense = jnp.einsum("rkos,rkn->rons", outlier_values, onehot, preferred_element_type=jnp.float32)
    dense = dense.reshape(block_rows, points)
    diff = snapshots.astype(jnp.float32) - dense
    return (jnp.sign(diff) * jnp.maximum(jnp.abs(diff) - threshold, 0.0)).astype(jnp.bfloat16)


def ring(cleaned):
    kept = [tile_product(cleaned, cleaned)]
    moving = cleaned
    for step in range(lax.axis_size("tm") // 2):
        moving = passed_along(moving, "tm", -1)
        kept.append(tile_product(cleaned, moving))
    return lax.psum_scatter(jnp.stack(kept, axis=1), "space", scatter_dimension=2, tiled=True)


def in_order(body, out_shape, n_in, n_after=0):
    anywhere = pl.BlockSpec(memory_space=pl.ANY)
    whole = pl.BlockSpec(memory_space=pltpu.VMEM)
    return pl.pallas_call(
        body,
        out_shape=out_shape,
        in_specs=[whole] * n_in + [anywhere] * n_after,
        out_specs=jax.tree.map(lambda _: whole, out_shape),
        compiler_params=pltpu.CompilerParams(vmem_limit_bytes=40 << 20),
        cost_estimate=pl.CostEstimate(flops=1000, bytes_accessed=1000, transcendentals=0),
    )


def clean_kernel(
    cols_hbm, threshold_ref, snapshots_hbm, values_hbm, all_ref, *refs
):
    *sent_refs, cols_ref, snapshots_ref, values_ref, cols_sem, row_sems, value_sems = refs
    tile_rows, listed, height, _ = values_ref.shape
    width = height // UNITS
    threshold = threshold_ref[0]
    cols_copy = pltpu.make_async_copy(cols_hbm, cols_ref, cols_sem)
    cols_copy.start()
    row_copies, value_copies = [], []
    for g in range(tile_rows):
        rows = pl.ds(g * height, height)
        row_copies.append(pltpu.make_async_copy(snapshots_hbm.at[rows], snapshots_ref.at[rows], row_sems.at[g]))
        value_copies.append(pltpu.make_async_copy(values_hbm.at[g], values_ref.at[g], value_sems.at[g]))
        row_copies[-1].start()
        value_copies[-1].start()
    cols_copy.wait()

    def shrunk(d):
        return (d - jnp.clip(d, -threshold, threshold)).astype(jnp.bfloat16)

    for g in range(tile_rows):
        row_copies[g].wait()

        def put(unit, columns, value):
            all_ref[unit, g * width : (g + 1) * width, columns] = value
            for stage, sent_ref in enumerate(sent_refs):
                if unit in STAGES[stage]:
                    top = (unit - STAGES[stage][0]) * height + g * width
                    sent_ref[top : top + width, columns] = value

        for unit in range(UNITS):
            rows = slice(g * height + unit * width, g * height + (unit + 1) * width)
            put(unit, slice(None), shrunk(snapshots_ref[rows, :].astype(jnp.float32)))
        value_copies[g].wait()
        for k in range(listed):
            col = cols_ref[g, k]
            columns = pl.ds(pl.multiple_of(col * ST, ST), ST)
            for unit in range(UNITS):
                rows = slice(unit * width, (unit + 1) * width)
                total = values_ref[g, k, rows, :].astype(jnp.float32)
                for other in range(listed):
                    if other != k:
                        same = jnp.where(cols_ref[g, other] == col, 1.0, 0.0)
                        total = total + same * values_ref[g, other, rows, :].astype(jnp.float32)
                rows = slice(g * height + unit * width, g * height + (unit + 1) * width)
                put(unit, columns, shrunk(snapshots_ref[rows, columns].astype(jnp.float32) - total))


def clean_units(snapshots, outlier_cols, outlier_values, threshold, first):
    rows, points = snapshots.shape
    tile_rows = outlier_values.shape[0]
    length = rows // UNITS
    out_shape = [jax.ShapeDtypeStruct((UNITS, length, points), jnp.bfloat16)]
    out_shape += [jax.ShapeDtypeStruct((len(units) * length, points), jnp.bfloat16) for units in STAGES[:first]]
    hbm = pl.BlockSpec(memory_space=pltpu.HBM)
    stay_put = functools.partial(pltpu.with_memory_space_constraint, memory_space=pltpu.HBM)
    return pl.pallas_call(
        clean_kernel,
        out_shape=out_shape,
        in_specs=[hbm, pl.BlockSpec(memory_space=pltpu.SMEM), hbm, hbm],
        out_specs=[pl.BlockSpec(memory_space=pltpu.VMEM)] * len(out_shape),
        scratch_shapes=[
            pltpu.SMEM(outlier_cols.shape, jnp.int32),
            pltpu.VMEM(snapshots.shape, jnp.bfloat16),
            pltpu.VMEM(outlier_values.shape, jnp.bfloat16),
            pltpu.SemaphoreType.DMA,
            pltpu.SemaphoreType.DMA((tile_rows,)),
            pltpu.SemaphoreType.DMA((tile_rows,)),
        ],
        compiler_params=pltpu.CompilerParams(vmem_limit_bytes=40 << 20),
    )(stay_put(outlier_cols), threshold.reshape(1), stay_put(snapshots), stay_put(outlier_values))


def columns_of(ref):
    here = lax.axis_index("space")
    width = ref.shape[0] // 4
    return [ref[pl.ds(pl.multiple_of((here ^ q) * width, width), width), :] for q in (0, 2, 1, 3)]


def multiply(cols, rows, down, stay_ref, away_ref, places):
    cols = [piece for ref in cols for piece in columns_of(ref)]
    product = tile_product(jnp.concatenate(cols, axis=0), jnp.concatenate([ref[...] for ref in rows], axis=0)) * down
    width, length = stay_ref.shape[2:]
    for c, line in enumerate(places):
        for s, place in enumerate(line):
            for q in range(4):
                top = (c * 4 + q) * width
                block = product[top : top + width, s * length : (s + 1) * length]
                (stay_ref, stay_ref, away_ref, away_ref)[q][q % 2, place] = block


def own_kernel(down, all_ref, stay_ref, away_ref, copy_ref):
    units = [all_ref.at[s] for s in range(UNITS)]
    for c in range(UNITS):
        multiply([units[c]], units, down, stay_ref, away_ref, [[c * UNITS + s for s in range(UNITS)]])
    copy_ref[...] = all_ref[...]


def x_blocks(stage):
    fresh, before = STAGES[stage], range(STAGES[stage][0])
    return [(c, s) for c in fresh for s in [*before, *fresh]] + [(c, s) for c in before for s in fresh]


def y_blocks(stage):
    return [(c, s) for c in STAGES[stage] for s in range(UNITS)]


def stage_blocks(stage):
    names = [("near", key) for key in x_blocks(stage)] + [("cross", key) for key in x_blocks(stage)]
    return names + [("y", key) for key in y_blocks(stage)] + [("side", key) for key in y_blocks(stage)]


def stage_kernel(down, stage, n_after, *refs):
    refs = list(refs)

    def take(n):
        out, refs[:n] = refs[:n], []
        return out

    all_ref, sibling_ref, y_ref, y_other_ref = take(4)
    x_refs = take(stage + 1)
    left_before, cross_before = take(stage), take(stage)
    take(n_after)
    stay_ref, away_ref, left_ref, cross_ref, side_ref = take(5)
    core = lax.rem(lax.axis_index("tm"), 2)
    far = lax.rem(lax.div(lax.axis_index("tm"), 2), 2)
    fresh, before = STAGES[stage], STAGES[stage][0]
    first, count = fresh[0], len(fresh)
    length = all_ref.shape[1]

    def unit_of(ref, i):
        return ref.at[pl.ds(i * length, length)]

    def units_of(stage_refs):
        return [unit_of(ref, i) for s, ref in enumerate(stage_refs) for i in range(len(STAGES[s]))]

    for i, unit in enumerate(fresh):
        rows = slice(i * length, (i + 1) * length)

        @pl.when(far == 1)
        def _():
            left_ref[rows] = y_ref[rows]
            cross_ref[rows] = y_other_ref[rows]

        @pl.when(far == 0)
        def _():
            left_ref[rows] = all_ref[unit]
            cross_ref[rows] = sibling_ref[unit]

        @pl.when(core == 0)
        def _():
            side_ref[rows] = sibling_ref[unit]

        @pl.when(core == 1)
        def _():
            side_ref[rows] = y_other_ref[rows]

    place = {key: i for i, key in enumerate(stage_blocks(stage))}
    x_units = units_of(x_refs)
    left, cross = units_of([*left_before, left_ref]), units_of([*cross_before, cross_ref])
    n = first + count
    multiply(
        x_units[first:],
        left + cross,
        down,
        stay_ref,
        away_ref,
        [[place[name, (c, s)] for name in ("near", "cross") for s in range(n)] for c in fresh],
    )
    if before > 0:
        multiply(
            x_units[:first],
            left[first:] + cross[first:],
            down,
            stay_ref,
            away_ref,
            [[place[name, (c, s)] for name in ("near", "cross") for s in fresh] for c in range(before)],
        )
    multiply(
        [unit_of(ref, i) for ref in (y_ref, side_ref) for i in range(count)],
        [all_ref.at[s] for s in range(UNITS)],
        down,
        stay_ref,
        away_ref,
        [[place[name, (c, s)] for s in range(UNITS)] for name in ("y", "side") for c in fresh],
    )


def assemble_kernel(scale, *refs):
    own_ref, out_ref = refs[0], refs[-1]
    core = lax.rem(lax.axis_index("tm"), 2)
    where = {("own", (c, s)): (own_ref, c * UNITS + s) for c in range(UNITS) for s in range(UNITS)}
    rest = iter(refs[1:-1])
    for first, last in GOES:
        for name in ("near", "cross"):
            keys = [key for stage in range(first, last) for key in x_blocks(stage)]
            ref = next(rest)
            where.update({(name, key): (ref, i) for i, key in enumerate(keys)})
    for stage in range(len(STAGES)):
        ref = next(rest)
        keys = [(name, key) for name in ("y", "side") for key in y_blocks(stage)]
        where.update({key: (ref, i) for i, key in enumerate(keys)})
    width = own_ref.shape[1]
    quarter = width * UNITS

    def put(k, name):
        for s in range(UNITS):
            pieces = [where[name, (c, s)] for c in range(UNITS)]
            tile = jnp.concatenate([ref[i] for ref, i in pieces], axis=0).T * scale
            for g in range(4):
                out_ref[k, g * quarter + s * width : g * quarter + (s + 1) * width, :] = tile[g * width : (g + 1) * width]

    put(0, "own")
    put(2, "near")
    put(4, "y")

    @pl.when(core == 0)
    def _():
        put(1, "side")
        put(3, "cross")

    @pl.when(core == 1)
    def _():
        put(1, "cross")
        put(3, "side")


def square(snapshots, outlier_cols, outlier_values, threshold):
    rows, points = snapshots.shape
    width, length = rows // (4 * UNITS), rows // UNITS
    far = (lax.axis_index("tm") // 2) % 2
    most = SNAP_MAX + outlier_cols.shape[1] * OUTLIER_MAX
    down = 2.0 ** -max(0, math.ceil(math.log2(2 * points * most * most / 6e4)))
    scale = 1.0 / (math.sqrt(points * lax.axis_size("space")) * down)

    def message(blocks):
        return [jax.ShapeDtypeStruct((2, blocks, width, length), jnp.float32)] * 2

    def units(n):
        return jax.ShapeDtypeStruct((n * length, points), jnp.bfloat16)

    def half_summed(stay, away):
        return stay + swapped(away.astype(jnp.float16), "space", 1).astype(jnp.float32)

    def summed(kept):
        return kept[0] + swapped(kept[1].astype(jnp.float16), "space", 2).astype(jnp.float32)

    whole, *sent = clean_units(snapshots, outlier_cols, outlier_values, threshold, len(STAGES))
    out_shape = message(UNITS * UNITS) + [jax.ShapeDtypeStruct(whole.shape, whole.dtype)]
    stay, away, lent = in_order(functools.partial(own_kernel, down), out_shape, 1)(whole)
    sibling = swapped(lent, "tm", 1)
    halves = [half_summed(stay, away)]
    own = summed(halves[0])
    x_units, left, cross, totals = [], [], [], []
    for stage, fresh in enumerate(STAGES):
        block = sent[stage]
        if stage > 0:
            block, *_ = lax.optimization_barrier((block, x_units[-1], y_units))
        x_units.append(swapped(block, "tm", 2))
        y_units = swapped(block, "tm", 4)
        y_other = swapped(lax.optimization_barrier((y_units, x_units[-1]))[0], "tm", 1)
        operands = [whole, sibling, y_units, y_other, *x_units, *left, *cross]
        after = [own] if stage == 1 else totals[:-1] if stage > 1 else []
        after = after + halves[-1:]
        out_shape = message(len(stage_blocks(stage))) + [units(len(fresh))] * 3
        stay, away, left_now, cross_now, _ = in_order(
            functools.partial(stage_kernel, down, stage, len(after)), out_shape, len(operands), len(after)
        )(*operands, *after)
        left.append(left_now)
        cross.append(cross_now)
        halves.append(half_summed(stay, away))
        totals.append(summed(halves[-1]))

    parts = []
    for first, last in GOES:
        near, other = [], []
        for stage in range(first, last):
            n = len(x_blocks(stage))
            near.append(totals[stage][:n])
            other.append(totals[stage][n : 2 * n])
        near, other = jnp.concatenate(near), jnp.concatenate(other)
        handed = swapped(near.astype(jnp.float16), "tm", 4, lambda i: i & 2)
        parts.append(jnp.where(far == 1, handed.astype(jnp.float32), near))
        pairs = [(i, i ^ (5 if i & 2 else 1)) for i in range(lax.axis_size("tm"))]
        parts.append(lax.ppermute(other.astype(jnp.float16), "tm", pairs).astype(jnp.float32))
    parts += [total[2 * len(x_blocks(stage)) :] for stage, total in enumerate(totals)]
    out_shape = jax.ShapeDtypeStruct((5, rows, rows // 4), jnp.float32)
    operands = [own, *parts]
    band = in_order(functools.partial(assemble_kernel, scale), out_shape, len(operands))(*operands)
    return band.transpose(1, 0, 2)


def local(snapshots, outlier_cols, outlier_values, threshold):
    if lax.axis_size("tm") == 8 and lax.axis_size("space") == 4:
        return square(snapshots, outlier_cols, outlier_values, threshold)
    points = snapshots.shape[1] * lax.axis_size("space")
    band = ring(clean(snapshots, outlier_cols, outlier_values, threshold))
    return band * (1.0 / jnp.sqrt(jnp.float32(points)))


def solution(mesh):
    placed = (P("tm", "space"), P("tm", "space"), P("tm", "space", None, None), P())
    return jax.shard_map(
        local, mesh=mesh, in_specs=placed, out_specs=P("tm", None, "space"), check_vma=False
    )
```

```python
import functools
import math

import jax
import jax.numpy as jnp
from jax import lax
from jax.experimental import pallas as pl
from jax.experimental.pallas import tpu as pltpu
from jax.sharding import PartitionSpec as P

ST = 128
SNAP_MAX = 6.0
OUTLIER_MAX = 12.0
UNITS = 4
GOES = ((0, UNITS - 1), (UNITS - 1, UNITS + 1))


def swapped(x, axis, bit, only=None):
    pairs = [(i, i ^ bit) for i in range(lax.axis_size(axis)) if only is None or only(i)]
    return lax.ppermute(x, axis, pairs)


def passed_along(x, axis, by):
    size = lax.axis_size(axis)
    return lax.ppermute(x, axis, [(i, (i + by) % size) for i in range(size)])


def tile_product(own, other):
    return lax.dot_general(own, other, (((1,), (1,)), ((), ())), preferred_element_type=jnp.float32)


def clean(snapshots, outlier_cols, outlier_values, threshold):
    block_rows, points = snapshots.shape
    tiles_dev = points // ST
    onehot = (
        outlier_cols[:, :, None] == jnp.arange(tiles_dev, dtype=jnp.int32)[None, None, :]
    ).astype(jnp.bfloat16)
    dense = jnp.einsum("rkos,rkn->rons", outlier_values, onehot, preferred_element_type=jnp.float32)
    dense = dense.reshape(block_rows, points)
    diff = snapshots.astype(jnp.float32) - dense
    return (jnp.sign(diff) * jnp.maximum(jnp.abs(diff) - threshold, 0.0)).astype(jnp.bfloat16)


def ring(cleaned):
    kept = [tile_product(cleaned, cleaned)]
    moving = cleaned
    for step in range(lax.axis_size("tm") // 2):
        moving = passed_along(moving, "tm", -1)
        kept.append(tile_product(cleaned, moving))
    return lax.psum_scatter(jnp.stack(kept, axis=1), "space", scatter_dimension=2, tiled=True)


def on_units(body, out_shape, n_in):
    whole = pl.BlockSpec(memory_space=pltpu.VMEM)
    return pl.pallas_call(
        body,
        out_shape=out_shape,
        in_specs=[whole] * n_in,
        out_specs=jax.tree.map(lambda _: whole, out_shape),
        compiler_params=pltpu.CompilerParams(vmem_limit_bytes=18 << 20),
        cost_estimate=pl.CostEstimate(flops=1000, bytes_accessed=1000, transcendentals=0),
    )


def clean_kernel(
    cols_hbm, threshold_ref, snapshots_hbm, values_hbm, all_ref, rest_ref, *refs
):
    *sent_refs, cols_ref, snapshots_ref, values_ref, cols_sem, row_sems, value_sems = refs
    tile_rows, listed, height, _ = values_ref.shape
    width = height // UNITS
    threshold = threshold_ref[0]
    cols_copy = pltpu.make_async_copy(cols_hbm, cols_ref, cols_sem)
    cols_copy.start()
    row_copies, value_copies = [], []
    for g in range(tile_rows):
        rows = pl.ds(g * height, height)
        row_copies.append(pltpu.make_async_copy(snapshots_hbm.at[rows], snapshots_ref.at[rows], row_sems.at[g]))
        value_copies.append(pltpu.make_async_copy(values_hbm.at[g], values_ref.at[g], value_sems.at[g]))
        row_copies[-1].start()
        value_copies[-1].start()
    cols_copy.wait()

    def shrunk(d):
        return (d - jnp.clip(d, -threshold, threshold)).astype(jnp.bfloat16)

    for g in range(tile_rows):
        row_copies[g].wait()

        def put(unit, columns, value):
            all_ref[unit, g * width : (g + 1) * width, columns] = value
            sent_refs[unit][g * width : (g + 1) * width, columns] = value
            if unit > 0:
                rest_ref[unit - 1, g * width : (g + 1) * width, columns] = value

        for unit in range(UNITS):
            rows = slice(g * height + unit * width, g * height + (unit + 1) * width)
            put(unit, slice(None), shrunk(snapshots_ref[rows, :].astype(jnp.float32)))
        value_copies[g].wait()
        for k in range(listed):
            col = cols_ref[g, k]
            columns = pl.ds(pl.multiple_of(col * ST, ST), ST)
            for unit in range(UNITS):
                rows = slice(unit * width, (unit + 1) * width)
                total = values_ref[g, k, rows, :].astype(jnp.float32)
                for other in range(listed):
                    if other != k:
                        same = jnp.where(cols_ref[g, other] == col, 1.0, 0.0)
                        total = total + same * values_ref[g, other, rows, :].astype(jnp.float32)
                rows = slice(g * height + unit * width, g * height + (unit + 1) * width)
                put(unit, columns, shrunk(snapshots_ref[rows, columns].astype(jnp.float32) - total))


def clean_units(snapshots, outlier_cols, outlier_values, threshold):
    rows, points = snapshots.shape
    tile_rows = outlier_values.shape[0]
    length = rows // UNITS
    out_shape = [jax.ShapeDtypeStruct((n, length, points), jnp.bfloat16) for n in (UNITS, UNITS - 1)]
    out_shape += [jax.ShapeDtypeStruct((length, points), jnp.bfloat16)] * UNITS
    hbm = pl.BlockSpec(memory_space=pltpu.HBM)
    stay_put = functools.partial(pltpu.with_memory_space_constraint, memory_space=pltpu.HBM)
    return pl.pallas_call(
        clean_kernel,
        out_shape=out_shape,
        in_specs=[hbm, pl.BlockSpec(memory_space=pltpu.SMEM), hbm, hbm],
        out_specs=[pl.BlockSpec(memory_space=pltpu.VMEM)] * len(out_shape),
        scratch_shapes=[
            pltpu.SMEM(outlier_cols.shape, jnp.int32),
            pltpu.VMEM(snapshots.shape, jnp.bfloat16),
            pltpu.VMEM(outlier_values.shape, jnp.bfloat16),
            pltpu.SemaphoreType.DMA,
            pltpu.SemaphoreType.DMA((tile_rows,)),
            pltpu.SemaphoreType.DMA((tile_rows,)),
        ],
        compiler_params=pltpu.CompilerParams(vmem_limit_bytes=18 << 20),
    )(stay_put(outlier_cols), threshold.reshape(1), stay_put(snapshots), stay_put(outlier_values))


def columns_of(ref):
    here = lax.axis_index("space")
    width = ref.shape[0] // 4
    return [ref[pl.ds(pl.multiple_of((here ^ q) * width, width), width), :] for q in (0, 2, 1, 3)]


def multiply(cols, rows, stay_ref, away_ref, places):
    cols = [piece for ref in cols for piece in columns_of(ref)]
    product = tile_product(jnp.concatenate(cols, axis=0), jnp.concatenate([ref[...] for ref in rows], axis=0))
    width, length = stay_ref.shape[2:]
    for c, line in enumerate(places):
        for s, place in enumerate(line):
            for q in range(4):
                top = (c * 4 + q) * width
                block = product[top : top + width, s * length : (s + 1) * length]
                (stay_ref, stay_ref, away_ref, away_ref)[q][q % 2, place] = block


def own_kernel(all_ref, stay_ref, away_ref):
    units = [all_ref.at[s] for s in range(UNITS)]
    for c in range(UNITS):
        multiply([units[c]], units, stay_ref, away_ref, [[c * UNITS + s for s in range(UNITS)]])


def x_blocks(unit):
    return [(unit, s) for s in range(unit + 1)] + [(c, unit) for c in range(unit)]


def message_blocks(step):
    fresh, late = step < UNITS, step > 0
    keys = [("near", key) for key in x_blocks(step)] * fresh + [("cross", key) for key in x_blocks(step - 1)] * late
    return keys + [("y", (step, s)) for s in range(UNITS)] * fresh + [("side", (step - 1, s)) for s in range(UNITS)] * late


def step_kernel(step, *refs):
    refs = list(refs)

    def take(n):
        out, refs[:n] = refs[:n], []
        return out

    fresh, late = step < UNITS, step > 0
    (all_ref,) = take(1)
    x_refs = take(min(step + 1, UNITS))
    y_ref = take(1)[0] if fresh else None
    sibling_ref, other_ref = take(2) if late else (None, None)
    left_refs, cross_refs = take(step if fresh else 0), take(step - 1 if late else 0)
    stay_ref, away_ref = take(2)
    core = lax.rem(lax.axis_index("tm"), 2)
    far = lax.rem(lax.div(lax.axis_index("tm"), 2), 2)
    units = [all_ref.at[s] for s in range(UNITS)]

    def choose(out_ref, flag, yes_ref, no_ref):
        @pl.when(flag == 1)
        def _():
            out_ref[...] = yes_ref[...]

        @pl.when(flag == 0)
        def _():
            out_ref[...] = no_ref[...]

    if fresh:
        left_refs += take(1)
        choose(left_refs[-1], far, y_ref, units[step])
    if late:
        cross_refs += take(1)
        (side_ref,) = take(1)
        if step > 1:
            sibling_ref = sibling_ref.at[step - 2]
        choose(cross_refs[-1], far, other_ref, sibling_ref)
        choose(side_ref, core, other_ref, sibling_ref)

    place = {key: i for i, key in enumerate(message_blocks(step))}

    def product(cols, rows):
        places = [[place[name, (c, s)] for name, s, _ in rows] for c, _ in cols]
        multiply([ref for _, ref in cols], [ref for *_, ref in rows], stay_ref, away_ref, places)

    x = list(enumerate(x_refs))
    left = [("near", s, ref) for s, ref in enumerate(left_refs)]
    cross = [("cross", s, ref) for s, ref in enumerate(cross_refs)]
    if fresh:
        product(x[step:], left)
    if late:
        product(x[step - 1 : step], left[step:] + cross)
    if step > 1:
        product(x[: step - 1], left[step:] + cross[step - 1 :])
    cols, places = [], []
    if fresh:
        cols.append(y_ref)
        places.append([place["y", (step, s)] for s in range(UNITS)])
    if late:
        cols.append(side_ref)
        places.append([place["side", (step - 1, s)] for s in range(UNITS)])
    multiply(cols, units, stay_ref, away_ref, places)


def pieces_of_result():
    pieces = []
    for first, last in GOES:
        for name in ("near", "cross"):
            pieces.append((name, [key for step in range(first, last) for key in message_blocks(step) if key[0] == name]))
    for step in range(UNITS + 1):
        pieces.append(("y", [key for key in message_blocks(step) if key[0] in ("y", "side")]))
    return pieces


def assemble_kernel(scale, *refs):
    own_ref, out_ref = refs[0], refs[-1]
    core = lax.rem(lax.axis_index("tm"), 2)
    where = {("own", (c, s)): (own_ref, c * UNITS + s) for c in range(UNITS) for s in range(UNITS)}
    for (_, keys), ref in zip(pieces_of_result(), refs[1:-1]):
        where.update({key: (ref, i) for i, key in enumerate(keys)})
    width = own_ref.shape[1]
    quarter = width * UNITS

    def put(k, name):
        for s in range(UNITS):
            pieces = [where[name, (c, s)] for c in range(UNITS)]
            tile = jnp.concatenate([ref[i] for ref, i in pieces], axis=0).T * scale
            for g in range(4):
                out_ref[k, g * quarter + s * width : g * quarter + (s + 1) * width, :] = tile[g * width : (g + 1) * width]

    put(0, "own")
    put(2, "near")
    put(4, "y")

    @pl.when(core == 0)
    def _():
        put(1, "side")
        put(3, "cross")

    @pl.when(core == 1)
    def _():
        put(1, "cross")
        put(3, "side")


def square(snapshots, outlier_cols, outlier_values, threshold):
    rows, points = snapshots.shape
    width, length = rows // (4 * UNITS), rows // UNITS
    far = (lax.axis_index("tm") // 2) % 2
    most = SNAP_MAX + outlier_cols.shape[1] * OUTLIER_MAX
    down = 2.0 ** -max(0, math.ceil(math.log2(2 * points * most * most / 6e4)))
    scale = 1.0 / (math.sqrt(points * lax.axis_size("space")) * down)

    def message(blocks):
        return [jax.ShapeDtypeStruct((2, blocks, width, length), jnp.float32)] * 2

    def units(n):
        return jax.ShapeDtypeStruct((n * length, points), jnp.bfloat16)

    def half_summed(stay, away):
        came = swapped((away * down).astype(jnp.float16), "space", 1)
        return stay * down + came.astype(jnp.float32), came

    def summed(kept, *others):
        came = swapped(behind(kept[1].astype(jnp.float16), *others), "space", 2)
        return kept[0] + came.astype(jnp.float32), came

    def behind(value, *others):
        return lax.optimization_barrier((value, *others))[0]

    whole, rest, *sent = clean_units(snapshots, outlier_cols, outlier_values, threshold)
    sibling = [swapped(sent[0], "tm", 1), swapped(rest, "tm", 1)]
    stay, away = on_units(own_kernel, message(UNITS * UNITS), 1)(behind(whole, sibling[0]))
    own_half, own_came = half_summed(stay, away)
    own, _ = summed(own_half)
    x_units, by_y, left, cross, totals, kept, other = [], [], [], [], [], [], None
    came = []
    came_last = []
    for step in range(UNITS + 1):
        fresh, late = step < UNITS, step > 0
        if fresh:
            block = sent[step]
            if step > 1:
                seen = 0 if step == 2 else step - 1
                block = behind(block, x_units[seen], by_y[seen])
            x_units.append(swapped(block, "tm", 2))
            by_y.append(swapped(block, "tm", 4))
        whole = behind(whole, *((own_came,), came_last, came_last, came[-1:], left[-1:])[step])
        operands = [whole, *x_units] + by_y[step:] + ([sibling[step > 1], other] if late else [])
        operands += (left if fresh else []) + cross
        out_shape = message(len(message_blocks(step))) + [units(1)] * (fresh + 2 * late)
        stay, away, *chosen = on_units(
            functools.partial(step_kernel, step), out_shape, len(operands)
        )(*operands)
        if fresh:
            left.append(chosen[0])
            other = swapped(behind(by_y[step], x_units[step], *came[-1:]), "tm", 1)
        if late:
            cross.append(chosen[-2])
        half, arrived = half_summed(stay, away)
        came.append(arrived)
        kept.append(half)
        if step < UNITS - 1:
            total, last = summed(half)
            totals.append(total)
            came_last = [last]
    totals += [summed(kept[-2], stay)[0], summed(kept[-1])[0]]

    def blocks_of(step, names):
        taken = [i for i, key in enumerate(message_blocks(step)) if key[0] in names]
        runs = [i for i in taken if i - 1 not in taken]
        return [totals[step][i : next(j for j in range(i, i + len(taken) + 1) if j not in taken)] for i in runs]

    parts = []
    for first, last in GOES:
        near = jnp.concatenate([part for step in range(first, last) for part in blocks_of(step, ("near",))])
        cross = jnp.concatenate([part for step in range(first, last) for part in blocks_of(step, ("cross",))])
        near, cross = (behind(part, *(parts or came[-2:-1])) for part in (near, cross))
        handed = swapped(near.astype(jnp.float16), "tm", 4, lambda i: i & 2)
        parts.append(jnp.where(far == 1, handed.astype(jnp.float32), near))
        pairs = [(i, i ^ (5 if i & 2 else 1)) for i in range(lax.axis_size("tm"))]
        parts.append(lax.ppermute(cross.astype(jnp.float16), "tm", pairs).astype(jnp.float32))
    parts += [jnp.concatenate(blocks_of(step, ("y", "side"))) for step in range(UNITS + 1)]
    out_shape = jax.ShapeDtypeStruct((5, rows, rows // 4), jnp.float32)
    operands = [own, *parts]
    band = on_units(functools.partial(assemble_kernel, scale), out_shape, len(operands))(*operands)
    return band.transpose(1, 0, 2)


def local(snapshots, outlier_cols, outlier_values, threshold):
    if lax.axis_size("tm") == 8 and lax.axis_size("space") == 4:
        return square(snapshots, outlier_cols, outlier_values, threshold)
    points = snapshots.shape[1] * lax.axis_size("space")
    band = ring(clean(snapshots, outlier_cols, outlier_values, threshold))
    return band * (1.0 / jnp.sqrt(jnp.float32(points)))


def solution(mesh):
    placed = (P("tm", "space"), P("tm", "space"), P("tm", "space", None, None), P())
    return jax.shard_map(
        local, mesh=mesh, in_specs=placed, out_specs=P("tm", None, "space"), check_vma=False
    )
```

```python
import functools
import math

import jax
import jax.numpy as jnp
from jax import lax
from jax.experimental import pallas as pl
from jax.experimental.pallas import tpu as pltpu
from jax.sharding import PartitionSpec as P

ST = 128
SNAP_MAX = 6.0
OUTLIER_MAX = 12.0
UNITS = 4
STAGES = ((0, 1), (2,), (3,))
GOES = ((0, 2), (2, 3))


def swapped(x, axis, bit, only=None):
    pairs = [(i, i ^ bit) for i in range(lax.axis_size(axis)) if only is None or only(i)]
    return lax.ppermute(x, axis, pairs)


def passed_along(x, axis, by):
    size = lax.axis_size(axis)
    return lax.ppermute(x, axis, [(i, (i + by) % size) for i in range(size)])


def tile_product(own, other):
    return lax.dot_general(own, other, (((1,), (1,)), ((), ())), preferred_element_type=jnp.float32)


def clean(snapshots, outlier_cols, outlier_values, threshold):
    block_rows, points = snapshots.shape
    tiles_dev = points // ST
    onehot = (
        outlier_cols[:, :, None] == jnp.arange(tiles_dev, dtype=jnp.int32)[None, None, :]
    ).astype(jnp.bfloat16)
    dense = jnp.einsum("rkos,rkn->rons", outlier_values, onehot, preferred_element_type=jnp.float32)
    dense = dense.reshape(block_rows, points)
    diff = snapshots.astype(jnp.float32) - dense
    return (jnp.sign(diff) * jnp.maximum(jnp.abs(diff) - threshold, 0.0)).astype(jnp.bfloat16)


def ring(cleaned):
    kept = [tile_product(cleaned, cleaned)]
    moving = cleaned
    for step in range(lax.axis_size("tm") // 2):
        moving = passed_along(moving, "tm", -1)
        kept.append(tile_product(cleaned, moving))
    return lax.psum_scatter(jnp.stack(kept, axis=1), "space", scatter_dimension=2, tiled=True)


def on_units(body, out_shape, n_in):
    whole = pl.BlockSpec(memory_space=pltpu.VMEM)
    return pl.pallas_call(
        body,
        out_shape=out_shape,
        in_specs=[whole] * n_in,
        out_specs=jax.tree.map(lambda _: whole, out_shape),
        compiler_params=pltpu.CompilerParams(vmem_limit_bytes=18 << 20),
        cost_estimate=pl.CostEstimate(flops=1000, bytes_accessed=1000, transcendentals=0),
    )


def clean_kernel(
    cols_hbm, threshold_ref, snapshots_hbm, values_hbm, rest_ref, *refs
):
    *sent_refs, cols_ref, snapshots_ref, values_ref, cols_sem, row_sems, value_sems = refs
    tile_rows, listed, height, _ = values_ref.shape
    width = height // UNITS
    threshold = threshold_ref[0]
    cols_copy = pltpu.make_async_copy(cols_hbm, cols_ref, cols_sem)
    cols_copy.start()
    row_copies, value_copies = [], []
    for g in range(tile_rows):
        rows = pl.ds(g * height, height)
        row_copies.append(pltpu.make_async_copy(snapshots_hbm.at[rows], snapshots_ref.at[rows], row_sems.at[g]))
        value_copies.append(pltpu.make_async_copy(values_hbm.at[g], values_ref.at[g], value_sems.at[g]))
        row_copies[-1].start()
        value_copies[-1].start()
    cols_copy.wait()

    def shrunk(d):
        return (d - jnp.clip(d, -threshold, threshold)).astype(jnp.bfloat16)

    for g in range(tile_rows):
        row_copies[g].wait()

        def put(unit, columns, value):
            if unit >= len(STAGES[0]):
                top = (unit - len(STAGES[0])) * height + g * width
                rest_ref[top : top + width, columns] = value
            for stage, sent_ref in enumerate(sent_refs):
                if unit in STAGES[stage]:
                    top = (unit - STAGES[stage][0]) * height + g * width
                    sent_ref[top : top + width, columns] = value

        for unit in range(UNITS):
            rows = slice(g * height + unit * width, g * height + (unit + 1) * width)
            put(unit, slice(None), shrunk(snapshots_ref[rows, :].astype(jnp.float32)))
        value_copies[g].wait()
        for k in range(listed):
            col = cols_ref[g, k]
            columns = pl.ds(pl.multiple_of(col * ST, ST), ST)
            for unit in range(UNITS):
                rows = slice(unit * width, (unit + 1) * width)
                total = values_ref[g, k, rows, :].astype(jnp.float32)
                for other in range(listed):
                    if other != k:
                        same = jnp.where(cols_ref[g, other] == col, 1.0, 0.0)
                        total = total + same * values_ref[g, other, rows, :].astype(jnp.float32)
                rows = slice(g * height + unit * width, g * height + (unit + 1) * width)
                put(unit, columns, shrunk(snapshots_ref[rows, columns].astype(jnp.float32) - total))


def clean_units(snapshots, outlier_cols, outlier_values, threshold):
    rows, points = snapshots.shape
    tile_rows = outlier_values.shape[0]
    length = rows // UNITS
    counts = [UNITS - len(STAGES[0])] + [len(units) for units in STAGES]
    out_shape = [jax.ShapeDtypeStruct((n * length, points), jnp.bfloat16) for n in counts]
    hbm = pl.BlockSpec(memory_space=pltpu.HBM)
    stay_put = functools.partial(pltpu.with_memory_space_constraint, memory_space=pltpu.HBM)
    return pl.pallas_call(
        clean_kernel,
        out_shape=out_shape,
        in_specs=[hbm, pl.BlockSpec(memory_space=pltpu.SMEM), hbm, hbm],
        out_specs=[pl.BlockSpec(memory_space=pltpu.VMEM)] * len(out_shape),
        scratch_shapes=[
            pltpu.SMEM(outlier_cols.shape, jnp.int32),
            pltpu.VMEM(snapshots.shape, jnp.bfloat16),
            pltpu.VMEM(outlier_values.shape, jnp.bfloat16),
            pltpu.SemaphoreType.DMA,
            pltpu.SemaphoreType.DMA((tile_rows,)),
            pltpu.SemaphoreType.DMA((tile_rows,)),
        ],
        compiler_params=pltpu.CompilerParams(vmem_limit_bytes=18 << 20),
    )(stay_put(outlier_cols), threshold.reshape(1), stay_put(snapshots), stay_put(outlier_values))


def columns_of(ref):
    here = lax.axis_index("space")
    width = ref.shape[0] // 4
    return [ref[pl.ds(pl.multiple_of((here ^ q) * width, width), width), :] for q in (0, 2, 1, 3)]


def multiply(cols, rows, stay_ref, away_ref, places):
    cols = [piece for ref in cols for piece in columns_of(ref)]
    product = tile_product(jnp.concatenate(cols, axis=0), jnp.concatenate([ref[...] for ref in rows], axis=0))
    width, length = stay_ref.shape[2:]
    for c, line in enumerate(places):
        for s, place in enumerate(line):
            for q in range(4):
                top = (c * 4 + q) * width
                block = product[top : top + width, s * length : (s + 1) * length]
                (stay_ref, stay_ref, away_ref, away_ref)[q][q % 2, place] = block


def units_of(stage_refs):
    length = stage_refs[0].shape[0] // len(STAGES[0])
    return [ref.at[pl.ds(i * length, length)] for s, ref in enumerate(stage_refs) for i in range(len(STAGES[s]))]


def own_kernel(*refs):
    *own_refs, stay_ref, away_ref = refs
    units = units_of(own_refs)
    for c in range(UNITS):
        multiply([units[c]], units, stay_ref, away_ref, [[c * UNITS + s for s in range(UNITS)]])


def x_blocks(stage):
    fresh, before = STAGES[stage], range(STAGES[stage][0])
    return [(c, s) for c in fresh for s in [*before, *fresh]] + [(c, s) for c in before for s in fresh]


def y_blocks(stage):
    return [(c, s) for c in STAGES[stage] for s in range(UNITS)]


def stage_blocks(stage):
    names = [("near", key) for key in x_blocks(stage)] + [("cross", key) for key in x_blocks(stage)]
    return names + [("y", key) for key in y_blocks(stage)] + [("side", key) for key in y_blocks(stage)]


def stage_kernel(stage, *refs):
    refs = list(refs)

    def take(n):
        out, refs[:n] = refs[:n], []
        return out

    own_refs = take(len(STAGES))
    sibling_ref, y_ref, y_other_ref = take(3)
    x_refs = take(stage + 1)
    left_before, cross_before = take(stage), take(stage)
    stay_ref, away_ref, left_ref, cross_ref, side_ref = take(5)
    core = lax.rem(lax.axis_index("tm"), 2)
    far = lax.rem(lax.div(lax.axis_index("tm"), 2), 2)
    fresh, before = STAGES[stage], STAGES[stage][0]
    first, count = fresh[0], len(fresh)
    length = own_refs[0].shape[0] // len(STAGES[0])
    sibling_first = (first - len(STAGES[0])) * length if stage > 0 else 0

    def unit_of(ref, i):
        return ref.at[pl.ds(i * length, length)]

    for i in range(count):
        rows = slice(i * length, (i + 1) * length)
        sibling_rows = slice(sibling_first + i * length, sibling_first + (i + 1) * length)

        @pl.when(far == 1)
        def _():
            left_ref[rows] = y_ref[rows]
            cross_ref[rows] = y_other_ref[rows]

        @pl.when(far == 0)
        def _():
            left_ref[rows] = own_refs[stage][rows]
            cross_ref[rows] = sibling_ref[sibling_rows]

        @pl.when(core == 0)
        def _():
            side_ref[rows] = sibling_ref[sibling_rows]

        @pl.when(core == 1)
        def _():
            side_ref[rows] = y_other_ref[rows]

    place = {key: i for i, key in enumerate(stage_blocks(stage))}
    x_units = units_of(x_refs)
    left, cross = units_of([*left_before, left_ref]), units_of([*cross_before, cross_ref])
    n = first + count
    multiply(
        x_units[first:],
        left + cross,
        stay_ref,
        away_ref,
        [[place[name, (c, s)] for name in ("near", "cross") for s in range(n)] for c in fresh],
    )
    if before > 0:
        multiply(
            x_units[:first],
            left[first:] + cross[first:],
            stay_ref,
            away_ref,
            [[place[name, (c, s)] for name in ("near", "cross") for s in fresh] for c in range(before)],
        )
    multiply(
        [unit_of(ref, i) for ref in (y_ref, side_ref) for i in range(count)],
        units_of(own_refs),
        stay_ref,
        away_ref,
        [[place[name, (c, s)] for s in range(UNITS)] for name in ("y", "side") for c in fresh],
    )


def assemble_kernel(scale, *refs):
    own_ref, out_ref = refs[0], refs[-1]
    core = lax.rem(lax.axis_index("tm"), 2)
    where = {("own", (c, s)): (own_ref, c * UNITS + s) for c in range(UNITS) for s in range(UNITS)}
    rest = iter(refs[1:-1])
    for first, last in GOES:
        for name in ("near", "cross"):
            keys = [key for stage in range(first, last) for key in x_blocks(stage)]
            ref = next(rest)
            where.update({(name, key): (ref, i) for i, key in enumerate(keys)})
    for stage in range(len(STAGES)):
        ref = next(rest)
        keys = [(name, key) for name in ("y", "side") for key in y_blocks(stage)]
        where.update({key: (ref, i) for i, key in enumerate(keys)})
    width = own_ref.shape[1]
    quarter = width * UNITS

    def put(k, name):
        for s in range(UNITS):
            pieces = [where[name, (c, s)] for c in range(UNITS)]
            tile = jnp.concatenate([ref[i] for ref, i in pieces], axis=0).T * scale
            for g in range(4):
                out_ref[k, g * quarter + s * width : g * quarter + (s + 1) * width, :] = tile[g * width : (g + 1) * width]

    put(0, "own")
    put(2, "near")
    put(4, "y")

    @pl.when(core == 0)
    def _():
        put(1, "side")
        put(3, "cross")

    @pl.when(core == 1)
    def _():
        put(1, "cross")
        put(3, "side")


def square(snapshots, outlier_cols, outlier_values, threshold):
    rows, points = snapshots.shape
    width, length = rows // (4 * UNITS), rows // UNITS
    far = (lax.axis_index("tm") // 2) % 2
    most = SNAP_MAX + outlier_cols.shape[1] * OUTLIER_MAX
    down = 2.0 ** -max(0, math.ceil(math.log2(2 * points * most * most / 6e4)))
    scale = 1.0 / (math.sqrt(points * lax.axis_size("space")) * down)

    def message(blocks):
        return [jax.ShapeDtypeStruct((2, blocks, width, length), jnp.float32)] * 2

    def units(n):
        return jax.ShapeDtypeStruct((n * length, points), jnp.bfloat16)

    def behind(value, *others):
        return lax.optimization_barrier((value, *others))[0]

    def half_summed(stay, away):
        came = swapped((away * down).astype(jnp.float16), "space", 1)
        return stay * down + came.astype(jnp.float32), came

    def summed(kept):
        return kept[0] + swapped(kept[1].astype(jnp.float16), "space", 2).astype(jnp.float32)

    rest, *sent = clean_units(snapshots, outlier_cols, outlier_values, threshold)
    stay, away = on_units(own_kernel, message(UNITS * UNITS), len(sent))(*sent)
    sibling = swapped(sent[0], "tm", 1)
    half, own_came = half_summed(stay, away)
    own = summed(half)
    x_units, by_y, left, cross, totals, came = [], [], [], [], [], None
    for stage, fresh in enumerate(STAGES):
        block = sent[stage]
        if stage > 0:
            block = behind(block, x_units[-1], by_y[-1])
        x_units.append(swapped(block, "tm", 2))
        by_y.append(swapped(block, "tm", 4))
        other = swapped(behind(by_y[-1], x_units[-1], *([own_came], left, left[1:])[stage]), "tm", 1)
        if stage == 1:
            sibling = swapped(behind(rest, left[0]), "tm", 1)
        if stage > 0:
            other = behind(other, came, *([own] if stage == 1 else totals[:-1]))
        operands = [*sent, sibling, by_y[-1], other, *x_units, *left, *cross]
        out_shape = message(len(stage_blocks(stage))) + [units(len(fresh))] * 3
        stay, away, left_now, cross_now, _ = on_units(
            functools.partial(stage_kernel, stage), out_shape, len(operands)
        )(*operands)
        left.append(left_now)
        cross.append(cross_now)
        half, came = half_summed(stay, away)
        totals.append(summed(half))

    parts = []
    for first, last in GOES:
        near, other = [], []
        for stage in range(first, last):
            n = len(x_blocks(stage))
            near.append(totals[stage][:n])
            other.append(totals[stage][n : 2 * n])
        near, other = (behind(jnp.concatenate(part), *(parts or [came])) for part in (near, other))
        handed = swapped(near.astype(jnp.float16), "tm", 4, lambda i: i & 2)
        parts.append(jnp.where(far == 1, handed.astype(jnp.float32), near))
        pairs = [(i, i ^ (5 if i & 2 else 1)) for i in range(lax.axis_size("tm"))]
        parts.append(lax.ppermute(other.astype(jnp.float16), "tm", pairs).astype(jnp.float32))
    parts += [total[2 * len(x_blocks(stage)) :] for stage, total in enumerate(totals)]
    out_shape = jax.ShapeDtypeStruct((5, rows, rows // 4), jnp.float32)
    operands = [own, *parts]
    band = on_units(functools.partial(assemble_kernel, scale), out_shape, len(operands))(*operands)
    return band.transpose(1, 0, 2)


def local(snapshots, outlier_cols, outlier_values, threshold):
    if lax.axis_size("tm") == 8 and lax.axis_size("space") == 4:
        return square(snapshots, outlier_cols, outlier_values, threshold)
    points = snapshots.shape[1] * lax.axis_size("space")
    band = ring(clean(snapshots, outlier_cols, outlier_values, threshold))
    return band * (1.0 / jnp.sqrt(jnp.float32(points)))


def solution(mesh):
    placed = (P("tm", "space"), P("tm", "space"), P("tm", "space", None, None), P())
    return jax.shard_map(
        local, mesh=mesh, in_specs=placed, out_specs=P("tm", None, "space"), check_vma=False
    )
```

```python
import functools
import math

import jax
import jax.numpy as jnp
from jax import lax
from jax.experimental import pallas as pl
from jax.experimental.pallas import tpu as pltpu
from jax.sharding import PartitionSpec as P

ST = 128
SNAP_MAX = 6.0
OUTLIER_MAX = 12.0
UNITS = 4
STAGES = ((0, 1), (2,), (3,))


def swapped(x, axis, bit, only=None):
    pairs = [(i, i ^ bit) for i in range(lax.axis_size(axis)) if only is None or only(i)]
    return lax.ppermute(x, axis, pairs)


def passed_along(x, axis, by):
    size = lax.axis_size(axis)
    return lax.ppermute(x, axis, [(i, (i + by) % size) for i in range(size)])


def tile_product(own, other):
    return lax.dot_general(own, other, (((1,), (1,)), ((), ())), preferred_element_type=jnp.float32)


def clean(snapshots, outlier_cols, outlier_values, threshold):
    block_rows, points = snapshots.shape
    tiles_dev = points // ST
    onehot = (
        outlier_cols[:, :, None] == jnp.arange(tiles_dev, dtype=jnp.int32)[None, None, :]
    ).astype(jnp.bfloat16)
    dense = jnp.einsum("rkos,rkn->rons", outlier_values, onehot, preferred_element_type=jnp.float32)
    dense = dense.reshape(block_rows, points)
    diff = snapshots.astype(jnp.float32) - dense
    return (jnp.sign(diff) * jnp.maximum(jnp.abs(diff) - threshold, 0.0)).astype(jnp.bfloat16)


def ring(cleaned):
    kept = [tile_product(cleaned, cleaned)]
    moving = cleaned
    for step in range(lax.axis_size("tm") // 2):
        moving = passed_along(moving, "tm", -1)
        kept.append(tile_product(cleaned, moving))
    return lax.psum_scatter(jnp.stack(kept, axis=1), "space", scatter_dimension=2, tiled=True)


def on_units(body, out_shape, n_in):
    whole = pl.BlockSpec(memory_space=pltpu.VMEM)
    return pl.pallas_call(
        body,
        out_shape=out_shape,
        in_specs=[whole] * n_in,
        out_specs=jax.tree.map(lambda _: whole, out_shape),
        compiler_params=pltpu.CompilerParams(vmem_limit_bytes=18 << 20),
        cost_estimate=pl.CostEstimate(flops=1000, bytes_accessed=1000, transcendentals=0),
    )


def clean_kernel(
    cols_hbm, threshold_ref, snapshots_hbm, values_hbm, rest_ref, *refs
):
    *sent_refs, cols_ref, snapshots_ref, values_ref, cols_sem, row_sems, value_sems = refs
    tile_rows, listed, height, _ = values_ref.shape
    width = height // UNITS
    threshold = threshold_ref[0]
    cols_copy = pltpu.make_async_copy(cols_hbm, cols_ref, cols_sem)
    cols_copy.start()
    row_copies, value_copies = [], []
    for g in range(tile_rows):
        rows = pl.ds(g * height, height)
        row_copies.append(pltpu.make_async_copy(snapshots_hbm.at[rows], snapshots_ref.at[rows], row_sems.at[g]))
        value_copies.append(pltpu.make_async_copy(values_hbm.at[g], values_ref.at[g], value_sems.at[g]))
        row_copies[-1].start()
        value_copies[-1].start()
    cols_copy.wait()

    def shrunk(d):
        return (d - jnp.clip(d, -threshold, threshold)).astype(jnp.bfloat16)

    for g in range(tile_rows):
        row_copies[g].wait()

        def put(unit, columns, value):
            if unit >= len(STAGES[0]):
                top = (unit - len(STAGES[0])) * height + g * width
                rest_ref[top : top + width, columns] = value
            for stage, sent_ref in enumerate(sent_refs):
                if unit in STAGES[stage]:
                    top = (unit - STAGES[stage][0]) * height + g * width
                    sent_ref[top : top + width, columns] = value

        for unit in range(UNITS):
            rows = slice(g * height + unit * width, g * height + (unit + 1) * width)
            put(unit, slice(None), shrunk(snapshots_ref[rows, :].astype(jnp.float32)))
        value_copies[g].wait()
        for k in range(listed):
            col = cols_ref[g, k]
            columns = pl.ds(pl.multiple_of(col * ST, ST), ST)
            for unit in range(UNITS):
                rows = slice(unit * width, (unit + 1) * width)
                total = values_ref[g, k, rows, :].astype(jnp.float32)
                for other in range(listed):
                    if other != k:
                        same = jnp.where(cols_ref[g, other] == col, 1.0, 0.0)
                        total = total + same * values_ref[g, other, rows, :].astype(jnp.float32)
                rows = slice(g * height + unit * width, g * height + (unit + 1) * width)
                put(unit, columns, shrunk(snapshots_ref[rows, columns].astype(jnp.float32) - total))


def clean_units(snapshots, outlier_cols, outlier_values, threshold):
    rows, points = snapshots.shape
    tile_rows = outlier_values.shape[0]
    length = rows // UNITS
    counts = [UNITS - len(STAGES[0])] + [len(units) for units in STAGES]
    out_shape = [jax.ShapeDtypeStruct((n * length, points), jnp.bfloat16) for n in counts]
    hbm = pl.BlockSpec(memory_space=pltpu.HBM)
    stay_put = functools.partial(pltpu.with_memory_space_constraint, memory_space=pltpu.HBM)
    return pl.pallas_call(
        clean_kernel,
        out_shape=out_shape,
        in_specs=[hbm, pl.BlockSpec(memory_space=pltpu.SMEM), hbm, hbm],
        out_specs=[pl.BlockSpec(memory_space=pltpu.VMEM)] * len(out_shape),
        scratch_shapes=[
            pltpu.SMEM(outlier_cols.shape, jnp.int32),
            pltpu.VMEM(snapshots.shape, jnp.bfloat16),
            pltpu.VMEM(outlier_values.shape, jnp.bfloat16),
            pltpu.SemaphoreType.DMA,
            pltpu.SemaphoreType.DMA((tile_rows,)),
            pltpu.SemaphoreType.DMA((tile_rows,)),
        ],
        compiler_params=pltpu.CompilerParams(vmem_limit_bytes=18 << 20),
    )(stay_put(outlier_cols), threshold.reshape(1), stay_put(snapshots), stay_put(outlier_values))


def columns_of(ref):
    here = lax.axis_index("space")
    width = ref.shape[0] // 4
    return [ref[pl.ds(pl.multiple_of((here ^ q) * width, width), width), :] for q in (0, 2, 1, 3)]


def multiply(cols, rows, stay_ref, away_ref, places):
    cols = [piece for ref in cols for piece in columns_of(ref)]
    product = tile_product(jnp.concatenate(cols, axis=0), jnp.concatenate([ref[...] for ref in rows], axis=0))
    width, length = stay_ref.shape[2:]
    for c, line in enumerate(places):
        for s, place in enumerate(line):
            for q in range(4):
                top = (c * 4 + q) * width
                block = product[top : top + width, s * length : (s + 1) * length]
                (stay_ref, stay_ref, away_ref, away_ref)[q][q % 2, place] = block


def units_of(stage_refs):
    length = stage_refs[0].shape[0] // len(STAGES[0])
    return [ref.at[pl.ds(i * length, length)] for s, ref in enumerate(stage_refs) for i in range(len(STAGES[s]))]


def own_kernel(*refs):
    *own_refs, stay_ref, away_ref = refs
    units = units_of(own_refs)
    for c in range(UNITS):
        multiply([units[c]], units, stay_ref, away_ref, [[c * UNITS + s for s in range(UNITS)]])


def x_blocks(stage):
    fresh, before = STAGES[stage], range(STAGES[stage][0])
    return [(c, s) for c in fresh for s in [*before, *fresh]] + [(c, s) for c in before for s in fresh]


def y_blocks(stage):
    return [(c, s) for c in STAGES[stage] for s in range(UNITS)]


def stage_blocks(stage):
    names = [("near", key) for key in x_blocks(stage)] + [("cross", key) for key in x_blocks(stage)]
    return names + [("y", key) for key in y_blocks(stage)] + [("side", key) for key in y_blocks(stage)]


def stage_kernel(stage, *refs):
    refs = list(refs)

    def take(n):
        out, refs[:n] = refs[:n], []
        return out

    own_refs = take(len(STAGES))
    sibling_ref, y_ref, y_other_ref = take(3)
    x_refs = take(stage + 1)
    left_before, cross_before = take(stage), take(stage)
    stay_ref, away_ref, left_ref, cross_ref, side_ref = take(5)
    core = lax.rem(lax.axis_index("tm"), 2)
    far = lax.rem(lax.div(lax.axis_index("tm"), 2), 2)
    fresh, before = STAGES[stage], STAGES[stage][0]
    first, count = fresh[0], len(fresh)
    length = own_refs[0].shape[0] // len(STAGES[0])
    sibling_first = (first - len(STAGES[0])) * length if stage > 0 else 0

    def unit_of(ref, i):
        return ref.at[pl.ds(i * length, length)]

    for i in range(count):
        rows = slice(i * length, (i + 1) * length)
        sibling_rows = slice(sibling_first + i * length, sibling_first + (i + 1) * length)

        @pl.when(far == 1)
        def _():
            left_ref[rows] = y_ref[rows]
            cross_ref[rows] = y_other_ref[rows]

        @pl.when(far == 0)
        def _():
            left_ref[rows] = own_refs[stage][rows]
            cross_ref[rows] = sibling_ref[sibling_rows]

        @pl.when(core == 0)
        def _():
            side_ref[rows] = sibling_ref[sibling_rows]

        @pl.when(core == 1)
        def _():
            side_ref[rows] = y_other_ref[rows]

    place = {key: i for i, key in enumerate(stage_blocks(stage))}
    x_units = units_of(x_refs)
    left, cross = units_of([*left_before, left_ref]), units_of([*cross_before, cross_ref])
    n = first + count
    multiply(
        x_units[first:],
        left + cross,
        stay_ref,
        away_ref,
        [[place[name, (c, s)] for name in ("near", "cross") for s in range(n)] for c in fresh],
    )
    if before > 0:
        multiply(
            x_units[:first],
            left[first:] + cross[first:],
            stay_ref,
            away_ref,
            [[place[name, (c, s)] for name in ("near", "cross") for s in fresh] for c in range(before)],
        )
    multiply(
        [unit_of(ref, i) for ref in (y_ref, side_ref) for i in range(count)],
        units_of(own_refs),
        stay_ref,
        away_ref,
        [[place[name, (c, s)] for s in range(UNITS)] for name in ("y", "side") for c in fresh],
    )


def assemble_kernel(scale, own_ref, *refs):
    *total_refs, handed_ref, crossed_ref, out_ref = refs
    core = lax.rem(lax.axis_index("tm"), 2)
    far = lax.rem(lax.div(lax.axis_index("tm"), 2), 2)
    where = {("own", (c, s)): (own_ref, c * UNITS + s) for c in range(UNITS) for s in range(UNITS)}
    for stage, ref in enumerate(total_refs):
        where.update({key: (ref, i) for i, key in enumerate(stage_blocks(stage))})
    keys = [key for stage in range(len(STAGES)) for key in x_blocks(stage)]
    where.update({("handed", key): (handed_ref, i) for i, key in enumerate(keys)})
    where.update({("crossed", key): (crossed_ref, i) for i, key in enumerate(keys)})
    width = own_ref.shape[1]
    quarter = width * UNITS

    def put(k, name):
        for s in range(UNITS):
            pieces = [where[name, (c, s)] for c in range(UNITS)]
            tile = jnp.concatenate([ref[i] for ref, i in pieces], axis=0).T * scale
            for g in range(4):
                out_ref[k, g * quarter + s * width : g * quarter + (s + 1) * width, :] = tile[g * width : (g + 1) * width]

    put(0, "own")
    put(4, "y")

    @pl.when(far == 0)
    def _():
        put(2, "near")

    @pl.when(far == 1)
    def _():
        put(2, "handed")

    @pl.when(core == 0)
    def _():
        put(1, "side")
        put(3, "crossed")

    @pl.when(core == 1)
    def _():
        put(1, "crossed")
        put(3, "side")


def square(snapshots, outlier_cols, outlier_values, threshold):
    rows, points = snapshots.shape
    width, length = rows // (4 * UNITS), rows // UNITS
    most = SNAP_MAX + outlier_cols.shape[1] * OUTLIER_MAX
    down = 2.0 ** -max(0, math.ceil(math.log2(2 * points * most * most / 6e4)))
    scale = 1.0 / (math.sqrt(points * lax.axis_size("space")) * down)

    def message(blocks):
        return [jax.ShapeDtypeStruct((2, blocks, width, length), jnp.float32)] * 2

    def units(n):
        return jax.ShapeDtypeStruct((n * length, points), jnp.bfloat16)

    def behind(value, *others):
        return lax.optimization_barrier((value, *others))[0]

    def half_summed(stay, away):
        came = swapped((away * down).astype(jnp.float16), "space", 1)
        return stay * down + came.astype(jnp.float32), came

    def summed(kept):
        return kept[0] + swapped(kept[1].astype(jnp.float16), "space", 2).astype(jnp.float32)

    rest, *sent = clean_units(snapshots, outlier_cols, outlier_values, threshold)
    stay, away = on_units(own_kernel, message(UNITS * UNITS), len(sent))(*sent)
    sibling = swapped(sent[0], "tm", 1)
    half, own_came = half_summed(stay, away)
    own = summed(half)
    x_units, by_y, left, cross, totals, came = [], [], [], [], [], None
    for stage, fresh in enumerate(STAGES):
        block = sent[stage]
        if stage > 0:
            block = behind(block, x_units[-1], by_y[-1])
        x_units.append(swapped(block, "tm", 2))
        by_y.append(swapped(block, "tm", 4))
        other = swapped(behind(by_y[-1], x_units[-1], *([own_came, sibling], left, left[1:])[stage]), "tm", 1)
        if stage == 1:
            sibling = swapped(behind(rest, left[0]), "tm", 1)
        other = behind(other, *([], [came], [own, *totals[:-1]])[stage])
        operands = [*sent, sibling, by_y[-1], other, *x_units, *left, *cross]
        out_shape = message(len(stage_blocks(stage))) + [units(len(fresh))] * 3
        stay, away, left_now, cross_now, _ = on_units(
            functools.partial(stage_kernel, stage), out_shape, len(operands)
        )(*operands)
        left.append(left_now)
        cross.append(cross_now)
        half, came = half_summed(stay, away)
        totals.append(summed(half))

    counts = [len(x_blocks(stage)) for stage in range(len(STAGES))]
    near = jnp.concatenate([total[:n] for n, total in zip(counts, totals)]).astype(jnp.float16)
    crossing = jnp.concatenate([total[n : 2 * n] for n, total in zip(counts, totals)]).astype(jnp.float16)
    handed = swapped(near, "tm", 4, lambda i: i & 2)
    pairs = [(i, i ^ (5 if i & 2 else 1)) for i in range(lax.axis_size("tm"))]
    crossed = lax.ppermute(crossing, "tm", pairs)
    out_shape = jax.ShapeDtypeStruct((5, rows, rows // 4), jnp.float32)
    operands = [own, *totals, handed.astype(jnp.float32), crossed.astype(jnp.float32)]
    band = on_units(functools.partial(assemble_kernel, scale), out_shape, len(operands))(*operands)
    return band.transpose(1, 0, 2)


def local(snapshots, outlier_cols, outlier_values, threshold):
    if lax.axis_size("tm") == 8 and lax.axis_size("space") == 4:
        return square(snapshots, outlier_cols, outlier_values, threshold)
    points = snapshots.shape[1] * lax.axis_size("space")
    band = ring(clean(snapshots, outlier_cols, outlier_values, threshold))
    return band * (1.0 / jnp.sqrt(jnp.float32(points)))


def solution(mesh):
    placed = (P("tm", "space"), P("tm", "space"), P("tm", "space", None, None), P())
    return jax.shard_map(
        local, mesh=mesh, in_specs=placed, out_specs=P("tm", None, "space"), check_vma=False
    )
```

```python
import functools
import math

import jax
import jax.numpy as jnp
from jax import lax
from jax.experimental import pallas as pl
from jax.experimental.pallas import tpu as pltpu
from jax.sharding import PartitionSpec as P

ST = 128
SNAP_MAX = 6.0
OUTLIER_MAX = 12.0
UNITS = 4
STAGES = ((0, 1), (2,), (3,))


def swapped(x, axis, bit, only=None):
    pairs = [(i, i ^ bit) for i in range(lax.axis_size(axis)) if only is None or only(i)]
    return lax.ppermute(x, axis, pairs)


def passed_along(x, axis, by):
    size = lax.axis_size(axis)
    return lax.ppermute(x, axis, [(i, (i + by) % size) for i in range(size)])


def tile_product(own, other):
    return lax.dot_general(own, other, (((1,), (1,)), ((), ())), preferred_element_type=jnp.float32)


def clean(snapshots, outlier_cols, outlier_values, threshold):
    block_rows, points = snapshots.shape
    tiles_dev = points // ST
    onehot = (
        outlier_cols[:, :, None] == jnp.arange(tiles_dev, dtype=jnp.int32)[None, None, :]
    ).astype(jnp.bfloat16)
    dense = jnp.einsum("rkos,rkn->rons", outlier_values, onehot, preferred_element_type=jnp.float32)
    dense = dense.reshape(block_rows, points)
    diff = snapshots.astype(jnp.float32) - dense
    return (jnp.sign(diff) * jnp.maximum(jnp.abs(diff) - threshold, 0.0)).astype(jnp.bfloat16)


def ring(cleaned):
    kept = [tile_product(cleaned, cleaned)]
    moving = cleaned
    for step in range(lax.axis_size("tm") // 2):
        moving = passed_along(moving, "tm", -1)
        kept.append(tile_product(cleaned, moving))
    return lax.psum_scatter(jnp.stack(kept, axis=1), "space", scatter_dimension=2, tiled=True)


def on_units(body, out_shape, n_in):
    whole = pl.BlockSpec(memory_space=pltpu.VMEM)
    return pl.pallas_call(
        body,
        out_shape=out_shape,
        in_specs=[whole] * n_in,
        out_specs=jax.tree.map(lambda _: whole, out_shape),
        compiler_params=pltpu.CompilerParams(vmem_limit_bytes=18 << 20),
        cost_estimate=pl.CostEstimate(flops=1000, bytes_accessed=1000, transcendentals=0),
    )


def clean_kernel(
    cols_hbm, threshold_ref, snapshots_hbm, values_hbm, rest_ref, *refs
):
    *sent_refs, cols_ref, snapshots_ref, values_ref, cols_sem, row_sems, value_sems = refs
    tile_rows, listed, height, _ = values_ref.shape
    width = height // UNITS
    threshold = threshold_ref[0]
    cols_copy = pltpu.make_async_copy(cols_hbm, cols_ref, cols_sem)
    cols_copy.start()
    row_copies, value_copies = [], []
    for g in range(tile_rows):
        rows = pl.ds(g * height, height)
        row_copies.append(pltpu.make_async_copy(snapshots_hbm.at[rows], snapshots_ref.at[rows], row_sems.at[g]))
        value_copies.append(pltpu.make_async_copy(values_hbm.at[g], values_ref.at[g], value_sems.at[g]))
        row_copies[-1].start()
        value_copies[-1].start()
    cols_copy.wait()

    def shrunk(d):
        return (d - jnp.clip(d, -threshold, threshold)).astype(jnp.bfloat16)

    for g in range(tile_rows):
        row_copies[g].wait()

        def put(unit, columns, value):
            if unit >= len(STAGES[0]):
                top = (unit - len(STAGES[0])) * height + g * width
                rest_ref[top : top + width, columns] = value
            for stage, sent_ref in enumerate(sent_refs):
                if unit in STAGES[stage]:
                    top = (unit - STAGES[stage][0]) * height + g * width
                    sent_ref[top : top + width, columns] = value

        for unit in range(UNITS):
            rows = slice(g * height + unit * width, g * height + (unit + 1) * width)
            put(unit, slice(None), shrunk(snapshots_ref[rows, :].astype(jnp.float32)))
        value_copies[g].wait()
        for k in range(listed):
            col = cols_ref[g, k]
            columns = pl.ds(pl.multiple_of(col * ST, ST), ST)
            for unit in range(UNITS):
                rows = slice(unit * width, (unit + 1) * width)
                total = values_ref[g, k, rows, :].astype(jnp.float32)
                for other in range(listed):
                    if other != k:
                        same = jnp.where(cols_ref[g, other] == col, 1.0, 0.0)
                        total = total + same * values_ref[g, other, rows, :].astype(jnp.float32)
                rows = slice(g * height + unit * width, g * height + (unit + 1) * width)
                put(unit, columns, shrunk(snapshots_ref[rows, columns].astype(jnp.float32) - total))


def clean_units(snapshots, outlier_cols, outlier_values, threshold):
    rows, points = snapshots.shape
    tile_rows = outlier_values.shape[0]
    length = rows // UNITS
    counts = [UNITS - len(STAGES[0])] + [len(units) for units in STAGES]
    out_shape = [jax.ShapeDtypeStruct((n * length, points), jnp.bfloat16) for n in counts]
    hbm = pl.BlockSpec(memory_space=pltpu.HBM)
    stay_put = functools.partial(pltpu.with_memory_space_constraint, memory_space=pltpu.HBM)
    return pl.pallas_call(
        clean_kernel,
        out_shape=out_shape,
        in_specs=[hbm, pl.BlockSpec(memory_space=pltpu.SMEM), hbm, hbm],
        out_specs=[pl.BlockSpec(memory_space=pltpu.VMEM)] * len(out_shape),
        scratch_shapes=[
            pltpu.SMEM(outlier_cols.shape, jnp.int32),
            pltpu.VMEM(snapshots.shape, jnp.bfloat16),
            pltpu.VMEM(outlier_values.shape, jnp.bfloat16),
            pltpu.SemaphoreType.DMA,
            pltpu.SemaphoreType.DMA((tile_rows,)),
            pltpu.SemaphoreType.DMA((tile_rows,)),
        ],
        compiler_params=pltpu.CompilerParams(vmem_limit_bytes=18 << 20),
    )(stay_put(outlier_cols), threshold.reshape(1), stay_put(snapshots), stay_put(outlier_values))


def columns_of(ref):
    here = lax.axis_index("space")
    width = ref.shape[0] // 4
    return [ref[pl.ds(pl.multiple_of((here ^ q) * width, width), width), :] for q in (0, 2, 1, 3)]


def multiply(cols, rows, stay_ref, away_ref, places):
    cols = [piece for ref in cols for piece in columns_of(ref)]
    product = tile_product(jnp.concatenate(cols, axis=0), jnp.concatenate([ref[...] for ref in rows], axis=0))
    width, length = stay_ref.shape[2:]
    for c, line in enumerate(places):
        for s, place in enumerate(line):
            for q in range(4):
                top = (c * 4 + q) * width
                block = product[top : top + width, s * length : (s + 1) * length]
                (stay_ref, stay_ref, away_ref, away_ref)[q][q % 2, place] = block


def units_of(stage_refs):
    length = stage_refs[0].shape[0] // len(STAGES[0])
    return [ref.at[pl.ds(i * length, length)] for s, ref in enumerate(stage_refs) for i in range(len(STAGES[s]))]


def own_kernel(*refs):
    *own_refs, stay_ref, away_ref = refs
    units = units_of(own_refs)
    for c in range(UNITS):
        multiply([units[c]], units, stay_ref, away_ref, [[c * UNITS + s for s in range(UNITS)]])


def x_blocks(stage):
    fresh, before = STAGES[stage], range(STAGES[stage][0])
    return [(c, s) for c in fresh for s in [*before, *fresh]] + [(c, s) for c in before for s in fresh]


def y_blocks(stage):
    return [(c, s) for c in STAGES[stage] for s in range(UNITS)]


def stage_blocks(stage):
    names = [("near", key) for key in x_blocks(stage)] + [("cross", key) for key in x_blocks(stage)]
    return names + [("y", key) for key in y_blocks(stage)] + [("side", key) for key in y_blocks(stage)]


def stage_kernel(stage, *refs):
    refs = list(refs)

    def take(n):
        out, refs[:n] = refs[:n], []
        return out

    own_refs = take(len(STAGES))
    sibling_ref, y_ref, y_other_ref = take(3)
    x_refs = take(stage + 1)
    left_before, cross_before = take(stage), take(stage)
    stay_ref, away_ref, left_ref, cross_ref, side_ref = take(5)
    core = lax.rem(lax.axis_index("tm"), 2)
    far = lax.rem(lax.div(lax.axis_index("tm"), 2), 2)
    fresh, before = STAGES[stage], STAGES[stage][0]
    first, count = fresh[0], len(fresh)
    length = own_refs[0].shape[0] // len(STAGES[0])
    sibling_first = (first - len(STAGES[0])) * length if stage > 0 else 0

    def unit_of(ref, i):
        return ref.at[pl.ds(i * length, length)]

    for i in range(count):
        rows = slice(i * length, (i + 1) * length)
        sibling_rows = slice(sibling_first + i * length, sibling_first + (i + 1) * length)

        @pl.when(far == 1)
        def _():
            left_ref[rows] = y_ref[rows]
            cross_ref[rows] = y_other_ref[rows]

        @pl.when(far == 0)
        def _():
            left_ref[rows] = own_refs[stage][rows]
            cross_ref[rows] = sibling_ref[sibling_rows]

        @pl.when(core == 0)
        def _():
            side_ref[rows] = sibling_ref[sibling_rows]

        @pl.when(core == 1)
        def _():
            side_ref[rows] = y_other_ref[rows]

    place = {key: i for i, key in enumerate(stage_blocks(stage))}
    x_units = units_of(x_refs)
    left, cross = units_of([*left_before, left_ref]), units_of([*cross_before, cross_ref])
    n = first + count
    multiply(
        x_units[first:],
        left + cross,
        stay_ref,
        away_ref,
        [[place[name, (c, s)] for name in ("near", "cross") for s in range(n)] for c in fresh],
    )
    if before > 0:
        multiply(
            x_units[:first],
            left[first:] + cross[first:],
            stay_ref,
            away_ref,
            [[place[name, (c, s)] for name in ("near", "cross") for s in fresh] for c in range(before)],
        )
    multiply(
        [unit_of(ref, i) for ref in (y_ref, side_ref) for i in range(count)],
        units_of(own_refs),
        stay_ref,
        away_ref,
        [[place[name, (c, s)] for s in range(UNITS)] for name in ("y", "side") for c in fresh],
    )


def assemble_kernel(scale, own_ref, *refs):
    *total_refs, handed_ref, crossed_ref, handed_last_ref, crossed_last_ref, out_ref = refs
    core = lax.rem(lax.axis_index("tm"), 2)
    far = lax.rem(lax.div(lax.axis_index("tm"), 2), 2)
    where = {("own", (c, s)): (own_ref, c * UNITS + s) for c in range(UNITS) for s in range(UNITS)}
    for stage, ref in enumerate(total_refs):
        where.update({key: (ref, i) for i, key in enumerate(stage_blocks(stage))})
    for i, key in enumerate(x_blocks(0) + x_blocks(1)):
        where.update({("handed", key): (handed_ref, i), ("crossed", key): (crossed_ref, i)})
    for i, key in enumerate(x_blocks(2)):
        where.update({("handed", key): (handed_last_ref, i), ("crossed", key): (crossed_last_ref, i)})
    width = own_ref.shape[1]
    quarter = width * UNITS

    def put(k, name):
        for s in range(UNITS):
            pieces = [where[name, (c, s)] for c in range(UNITS)]
            tile = jnp.concatenate([ref[i] for ref, i in pieces], axis=0).T * scale
            for g in range(4):
                out_ref[k, g * quarter + s * width : g * quarter + (s + 1) * width, :] = tile[g * width : (g + 1) * width]

    put(0, "own")
    put(4, "y")

    @pl.when(far == 0)
    def _():
        put(2, "near")

    @pl.when(far == 1)
    def _():
        put(2, "handed")

    @pl.when(core == 0)
    def _():
        put(1, "side")
        put(3, "crossed")

    @pl.when(core == 1)
    def _():
        put(1, "crossed")
        put(3, "side")


def square(snapshots, outlier_cols, outlier_values, threshold):
    rows, points = snapshots.shape
    width, length = rows // (4 * UNITS), rows // UNITS
    most = SNAP_MAX + outlier_cols.shape[1] * OUTLIER_MAX
    down = 2.0 ** -max(0, math.ceil(math.log2(2 * points * most * most / 6e4)))
    scale = 1.0 / (math.sqrt(points * lax.axis_size("space")) * down)

    def message(blocks):
        return [jax.ShapeDtypeStruct((2, blocks, width, length), jnp.float32)] * 2

    def units(n):
        return jax.ShapeDtypeStruct((n * length, points), jnp.bfloat16)

    def behind(value, *others):
        return lax.optimization_barrier((value, *others))[0]

    def exchanged(away):
        return swapped((away * down).astype(jnp.float16), "space", 1)

    def half_summed(stay, came):
        return stay * down + came.astype(jnp.float32)

    def summed(kept, after=()):
        came = swapped(kept[1].astype(jnp.float16), "space", 2)
        return kept[0] + behind(came, *after).astype(jnp.float32)

    def handed_over(stages):
        counts = [len(x_blocks(stage)) for stage in stages]
        near = jnp.concatenate([totals[stage][:n] for n, stage in zip(counts, stages)]).astype(jnp.float16)
        cross = jnp.concatenate([totals[stage][n : 2 * n] for n, stage in zip(counts, stages)]).astype(jnp.float16)
        pairs = [(i, i ^ (5 if i & 2 else 1)) for i in range(lax.axis_size("tm"))]
        return [swapped(near, "tm", 4, lambda i: i & 2), lax.ppermute(cross, "tm", pairs)]

    rest, *sent = clean_units(snapshots, outlier_cols, outlier_values, threshold)
    stay, away = on_units(own_kernel, message(UNITS * UNITS), len(sent))(*sent)
    sibling = swapped(sent[0], "tm", 1)
    own_came = exchanged(away)
    own_half = half_summed(stay, own_came)
    x_units, by_y, left, cross, halves, totals, came = [], [], [], [], [], [], None
    for stage, fresh in enumerate(STAGES):
        block = sent[stage]
        if stage > 0:
            block = behind(block, x_units[-1], by_y[-1])
        x_units.append(swapped(block, "tm", 2))
        by_y.append(swapped(block, "tm", 4))
        other = swapped(behind(by_y[-1], x_units[-1], *([own_came, sibling], left, left[1:])[stage]), "tm", 1)
        if stage == 1:
            sibling = swapped(behind(rest, left[0]), "tm", 1)
        if stage == 2:
            own = summed(own_half, after=[came])
            totals.append(summed(halves[0], after=left[1:]))
            other = behind(other, own, *totals)
        elif stage == 1:
            other = behind(other, came)
        operands = [*sent, sibling, by_y[-1], other, *x_units, *left, *cross]
        out_shape = message(len(stage_blocks(stage))) + [units(len(fresh))] * 3
        stay, away, left_now, cross_now, _ = on_units(
            functools.partial(stage_kernel, stage), out_shape, len(operands)
        )(*operands)
        left.append(left_now)
        cross.append(cross_now)
        came = exchanged(away)
        halves.append(half_summed(stay, came))
    totals.append(summed(halves[1], after=[came]))
    parts = handed_over([0, 1])
    totals.append(summed(halves[2], after=parts))
    parts += handed_over([2])

    out_shape = jax.ShapeDtypeStruct((5, rows, rows // 4), jnp.float32)
    operands = [own, *totals, *(part.astype(jnp.float32) for part in parts)]
    band = on_units(functools.partial(assemble_kernel, scale), out_shape, len(operands))(*operands)
    return band.transpose(1, 0, 2)


def local(snapshots, outlier_cols, outlier_values, threshold):
    if lax.axis_size("tm") == 8 and lax.axis_size("space") == 4:
        return square(snapshots, outlier_cols, outlier_values, threshold)
    points = snapshots.shape[1] * lax.axis_size("space")
    band = ring(clean(snapshots, outlier_cols, outlier_values, threshold))
    return band * (1.0 / jnp.sqrt(jnp.float32(points)))


def solution(mesh):
    placed = (P("tm", "space"), P("tm", "space"), P("tm", "space", None, None), P())
    return jax.shard_map(
        local, mesh=mesh, in_specs=placed, out_specs=P("tm", None, "space"), check_vma=False
    )
```

```python
import functools
import math

import jax
import jax.numpy as jnp
from jax import lax
from jax.experimental import pallas as pl
from jax.experimental.pallas import tpu as pltpu
from jax.sharding import PartitionSpec as P

ST = 128
SNAP_MAX = 6.0
OUTLIER_MAX = 12.0
UNITS = 4
STAGES = ((0, 1), (2,), (3,))


def swapped(x, axis, bit, only=None):
    pairs = [(i, i ^ bit) for i in range(lax.axis_size(axis)) if only is None or only(i)]
    return lax.ppermute(x, axis, pairs)


def passed_along(x, axis, by):
    size = lax.axis_size(axis)
    return lax.ppermute(x, axis, [(i, (i + by) % size) for i in range(size)])


def tile_product(own, other):
    return lax.dot_general(own, other, (((1,), (1,)), ((), ())), preferred_element_type=jnp.float32)


def clean(snapshots, outlier_cols, outlier_values, threshold):
    block_rows, points = snapshots.shape
    tiles_dev = points // ST
    onehot = (
        outlier_cols[:, :, None] == jnp.arange(tiles_dev, dtype=jnp.int32)[None, None, :]
    ).astype(jnp.bfloat16)
    dense = jnp.einsum("rkos,rkn->rons", outlier_values, onehot, preferred_element_type=jnp.float32)
    dense = dense.reshape(block_rows, points)
    diff = snapshots.astype(jnp.float32) - dense
    return (jnp.sign(diff) * jnp.maximum(jnp.abs(diff) - threshold, 0.0)).astype(jnp.bfloat16)


def ring(cleaned):
    kept = [tile_product(cleaned, cleaned)]
    moving = cleaned
    for step in range(lax.axis_size("tm") // 2):
        moving = passed_along(moving, "tm", -1)
        kept.append(tile_product(cleaned, moving))
    return lax.psum_scatter(jnp.stack(kept, axis=1), "space", scatter_dimension=2, tiled=True)


def on_units(body, out_shape, n_in):
    whole = pl.BlockSpec(memory_space=pltpu.VMEM)
    return pl.pallas_call(
        body,
        out_shape=out_shape,
        in_specs=[whole] * n_in,
        out_specs=jax.tree.map(lambda _: whole, out_shape),
        compiler_params=pltpu.CompilerParams(vmem_limit_bytes=18 << 20),
        cost_estimate=pl.CostEstimate(flops=1000, bytes_accessed=1000, transcendentals=0),
    )


def clean_kernel(
    cols_hbm, threshold_ref, snapshots_hbm, values_hbm, rest_ref, *refs
):
    *sent_refs, cols_ref, snapshots_ref, values_ref, cols_sem, row_sems, value_sems = refs
    tile_rows, listed, height, _ = values_ref.shape
    width = height // UNITS
    threshold = threshold_ref[0]
    cols_copy = pltpu.make_async_copy(cols_hbm, cols_ref, cols_sem)
    cols_copy.start()
    row_copies, value_copies = [], []
    for g in range(tile_rows):
        rows = pl.ds(g * height, height)
        row_copies.append(pltpu.make_async_copy(snapshots_hbm.at[rows], snapshots_ref.at[rows], row_sems.at[g]))
        value_copies.append(pltpu.make_async_copy(values_hbm.at[g], values_ref.at[g], value_sems.at[g]))
        row_copies[-1].start()
        value_copies[-1].start()
    cols_copy.wait()

    def shrunk(d):
        return (d - jnp.clip(d, -threshold, threshold)).astype(jnp.bfloat16)

    for g in range(tile_rows):
        row_copies[g].wait()

        def put(unit, columns, value):
            if unit >= len(STAGES[0]):
                top = (unit - len(STAGES[0])) * height + g * width
                rest_ref[top : top + width, columns] = value
            for stage, sent_ref in enumerate(sent_refs):
                if unit in STAGES[stage]:
                    top = (unit - STAGES[stage][0]) * height + g * width
                    sent_ref[top : top + width, columns] = value

        for unit in range(UNITS):
            rows = slice(g * height + unit * width, g * height + (unit + 1) * width)
            put(unit, slice(None), shrunk(snapshots_ref[rows, :].astype(jnp.float32)))
        value_copies[g].wait()
        for k in range(listed):
            col = cols_ref[g, k]
            columns = pl.ds(pl.multiple_of(col * ST, ST), ST)
            for unit in range(UNITS):
                rows = slice(unit * width, (unit + 1) * width)
                total = values_ref[g, k, rows, :].astype(jnp.float32)
                for other in range(listed):
                    if other != k:
                        same = jnp.where(cols_ref[g, other] == col, 1.0, 0.0)
                        total = total + same * values_ref[g, other, rows, :].astype(jnp.float32)
                rows = slice(g * height + unit * width, g * height + (unit + 1) * width)
                put(unit, columns, shrunk(snapshots_ref[rows, columns].astype(jnp.float32) - total))


def clean_units(snapshots, outlier_cols, outlier_values, threshold):
    rows, points = snapshots.shape
    tile_rows = outlier_values.shape[0]
    length = rows // UNITS
    counts = [UNITS - len(STAGES[0])] + [len(units) for units in STAGES]
    out_shape = [jax.ShapeDtypeStruct((n * length, points), jnp.bfloat16) for n in counts]
    hbm = pl.BlockSpec(memory_space=pltpu.HBM)
    stay_put = functools.partial(pltpu.with_memory_space_constraint, memory_space=pltpu.HBM)
    return pl.pallas_call(
        clean_kernel,
        out_shape=out_shape,
        in_specs=[hbm, pl.BlockSpec(memory_space=pltpu.SMEM), hbm, hbm],
        out_specs=[pl.BlockSpec(memory_space=pltpu.VMEM)] * len(out_shape),
        scratch_shapes=[
            pltpu.SMEM(outlier_cols.shape, jnp.int32),
            pltpu.VMEM(snapshots.shape, jnp.bfloat16),
            pltpu.VMEM(outlier_values.shape, jnp.bfloat16),
            pltpu.SemaphoreType.DMA,
            pltpu.SemaphoreType.DMA((tile_rows,)),
            pltpu.SemaphoreType.DMA((tile_rows,)),
        ],
        compiler_params=pltpu.CompilerParams(vmem_limit_bytes=18 << 20),
    )(stay_put(outlier_cols), threshold.reshape(1), stay_put(snapshots), stay_put(outlier_values))


def columns_of(ref):
    here = lax.axis_index("space")
    width = ref.shape[0] // 4
    return [ref[pl.ds(pl.multiple_of((here ^ q) * width, width), width), :] for q in (0, 2, 1, 3)]


def multiply(cols, rows, stay_ref, away_ref, places):
    cols = [piece for ref in cols for piece in columns_of(ref)]
    product = tile_product(jnp.concatenate(cols, axis=0), jnp.concatenate([ref[...] for ref in rows], axis=0))
    width, length = stay_ref.shape[2:]
    for c, line in enumerate(places):
        for s, place in enumerate(line):
            for q in range(4):
                top = (c * 4 + q) * width
                block = product[top : top + width, s * length : (s + 1) * length]
                (stay_ref, stay_ref, away_ref, away_ref)[q][q % 2, place] = block


def units_of(stage_refs):
    length = stage_refs[0].shape[0] // len(STAGES[0])
    return [ref.at[pl.ds(i * length, length)] for s, ref in enumerate(stage_refs) for i in range(len(STAGES[s]))]


def own_kernel(*refs):
    *own_refs, stay_ref, away_ref = refs
    units = units_of(own_refs)
    for c in range(UNITS):
        multiply([units[c]], units, stay_ref, away_ref, [[c * UNITS + s for s in range(UNITS)]])


def x_blocks(stage):
    fresh, before = STAGES[stage], range(STAGES[stage][0])
    return [(c, s) for c in fresh for s in [*before, *fresh]] + [(c, s) for c in before for s in fresh]


def y_blocks(stage):
    return [(c, s) for c in STAGES[stage] for s in range(UNITS)]


def stage_blocks(stage):
    names = [("near", key) for key in x_blocks(stage)] + [("cross", key) for key in x_blocks(stage)]
    return names + [("y", key) for key in y_blocks(stage)] + [("side", key) for key in y_blocks(stage)]


def stage_kernel(stage, *refs):
    refs = list(refs)

    def take(n):
        out, refs[:n] = refs[:n], []
        return out

    own_refs = take(len(STAGES))
    sibling_refs = take(len(STAGES[0]) if stage == 0 else 1)
    y_ref, y_other_ref = take(2)
    x_refs = take(stage + 1)
    left_before, cross_before = take(stage), take(stage)
    stay_ref, away_ref, left_ref, cross_ref, side_ref = take(5)
    core = lax.rem(lax.axis_index("tm"), 2)
    far = lax.rem(lax.div(lax.axis_index("tm"), 2), 2)
    fresh, before = STAGES[stage], STAGES[stage][0]
    first, count = fresh[0], len(fresh)
    length = own_refs[0].shape[0] // len(STAGES[0])
    sibling_first = (first - len(STAGES[0])) * length if stage > 0 else 0

    def unit_of(ref, i):
        return ref.at[pl.ds(i * length, length)]

    for i in range(count):
        rows = slice(i * length, (i + 1) * length)
        if stage == 0:
            sibling_ref, sibling_rows = sibling_refs[i], slice(None)
        else:
            sibling_ref = sibling_refs[0]
            sibling_rows = slice(sibling_first + i * length, sibling_first + (i + 1) * length)

        @pl.when(far == 1)
        def _():
            left_ref[rows] = y_ref[rows]
            cross_ref[rows] = y_other_ref[rows]

        @pl.when(far == 0)
        def _():
            left_ref[rows] = own_refs[stage][rows]
            cross_ref[rows] = sibling_ref[sibling_rows]

        @pl.when(core == 0)
        def _():
            side_ref[rows] = sibling_ref[sibling_rows]

        @pl.when(core == 1)
        def _():
            side_ref[rows] = y_other_ref[rows]

    place = {key: i for i, key in enumerate(stage_blocks(stage))}
    x_units = units_of(x_refs)
    left, cross = units_of([*left_before, left_ref]), units_of([*cross_before, cross_ref])
    n = first + count
    multiply(
        x_units[first:],
        left + cross,
        stay_ref,
        away_ref,
        [[place[name, (c, s)] for name in ("near", "cross") for s in range(n)] for c in fresh],
    )
    if before > 0:
        multiply(
            x_units[:first],
            left[first:] + cross[first:],
            stay_ref,
            away_ref,
            [[place[name, (c, s)] for name in ("near", "cross") for s in fresh] for c in range(before)],
        )
    multiply(
        [unit_of(ref, i) for ref in (y_ref, side_ref) for i in range(count)],
        units_of(own_refs),
        stay_ref,
        away_ref,
        [[place[name, (c, s)] for s in range(UNITS)] for name in ("y", "side") for c in fresh],
    )


def assemble_kernel(scale, own_ref, *refs):
    *total_refs, handed_ref, crossed_ref, handed_last_ref, crossed_last_ref, out_ref = refs
    core = lax.rem(lax.axis_index("tm"), 2)
    far = lax.rem(lax.div(lax.axis_index("tm"), 2), 2)
    where = {("own", (c, s)): (own_ref, c * UNITS + s) for c in range(UNITS) for s in range(UNITS)}
    for stage, ref in enumerate(total_refs):
        where.update({key: (ref, i) for i, key in enumerate(stage_blocks(stage))})
    for i, key in enumerate(x_blocks(0) + x_blocks(1)):
        where.update({("handed", key): (handed_ref, i), ("crossed", key): (crossed_ref, i)})
    for i, key in enumerate(x_blocks(2)):
        where.update({("handed", key): (handed_last_ref, i), ("crossed", key): (crossed_last_ref, i)})
    width = own_ref.shape[1]
    quarter = width * UNITS

    def put(k, name):
        for s in range(UNITS):
            pieces = [where[name, (c, s)] for c in range(UNITS)]
            tile = jnp.concatenate([ref[i] for ref, i in pieces], axis=0).T * scale
            for g in range(4):
                out_ref[k, g * quarter + s * width : g * quarter + (s + 1) * width, :] = tile[g * width : (g + 1) * width]

    put(0, "own")
    put(4, "y")

    @pl.when(far == 0)
    def _():
        put(2, "near")

    @pl.when(far == 1)
    def _():
        put(2, "handed")

    @pl.when(core == 0)
    def _():
        put(1, "side")
        put(3, "crossed")

    @pl.when(core == 1)
    def _():
        put(1, "crossed")
        put(3, "side")


def square(snapshots, outlier_cols, outlier_values, threshold):
    rows, points = snapshots.shape
    width, length = rows // (4 * UNITS), rows // UNITS
    most = SNAP_MAX + outlier_cols.shape[1] * OUTLIER_MAX
    down = 2.0 ** -max(0, math.ceil(math.log2(2 * points * most * most / 6e4)))
    scale = 1.0 / (math.sqrt(points * lax.axis_size("space")) * down)

    def message(blocks):
        return [jax.ShapeDtypeStruct((2, blocks, width, length), jnp.float32)] * 2

    def units(n):
        return jax.ShapeDtypeStruct((n * length, points), jnp.bfloat16)

    def behind(value, *others):
        return lax.optimization_barrier((value, *others))[0]

    def exchanged(away):
        return swapped((away * down).astype(jnp.float16), "space", 1)

    def half_summed(stay, came):
        return stay * down + came.astype(jnp.float32)

    def summed(kept, after=()):
        came = swapped(kept[1].astype(jnp.float16), "space", 2)
        return kept[0] + behind(came, *after).astype(jnp.float32)

    def handed_over(stages):
        counts = [len(x_blocks(stage)) for stage in stages]
        near = jnp.concatenate([totals[stage][:n] for n, stage in zip(counts, stages)]).astype(jnp.float16)
        cross = jnp.concatenate([totals[stage][n : 2 * n] for n, stage in zip(counts, stages)]).astype(jnp.float16)
        pairs = [(i, i ^ (5 if i & 2 else 1)) for i in range(lax.axis_size("tm"))]
        return [swapped(near, "tm", 4, lambda i: i & 2), lax.ppermute(cross, "tm", pairs)]

    rest, *sent = clean_units(snapshots, outlier_cols, outlier_values, threshold)
    stay, away = on_units(own_kernel, message(UNITS * UNITS), len(sent))(*sent)
    own_came = exchanged(away)
    own = summed(half_summed(stay, own_came))
    sibling = [swapped(behind(sent[0][i * length : (i + 1) * length], own), "tm", 1) for i in range(len(STAGES[0]))]
    x_units, by_y, left, cross, halves, totals, came = [], [], [], [], [], [], None
    for stage, fresh in enumerate(STAGES):
        block = sent[stage]
        if stage > 0:
            block = behind(block, x_units[-1], by_y[-1])
        x_units.append(swapped(block, "tm", 2))
        by_y.append(swapped(block, "tm", 4))
        other = swapped(behind(by_y[-1], x_units[-1], *([own_came], left, left[1:])[stage]), "tm", 1)
        if stage == 1:
            sibling = [swapped(behind(rest, left[0]), "tm", 1)]
        if stage == 2:
            totals.append(summed(halves[0], after=left[1:]))
            other = behind(other, came, *totals)
        elif stage == 1:
            other = behind(other, came)
        operands = [*sent, *sibling, by_y[-1], other, *x_units, *left, *cross]
        out_shape = message(len(stage_blocks(stage))) + [units(len(fresh))] * 3
        stay, away, left_now, cross_now, _ = on_units(
            functools.partial(stage_kernel, stage), out_shape, len(operands)
        )(*operands)
        left.append(left_now)
        cross.append(cross_now)
        came = exchanged(away)
        halves.append(half_summed(stay, came))
    totals.append(summed(halves[1], after=[came]))
    parts = handed_over([0, 1])
    totals.append(summed(halves[2], after=parts))
    parts += handed_over([2])

    out_shape = jax.ShapeDtypeStruct((5, rows, rows // 4), jnp.float32)
    operands = [own, *totals, *(part.astype(jnp.float32) for part in parts)]
    band = on_units(functools.partial(assemble_kernel, scale), out_shape, len(operands))(*operands)
    return band.transpose(1, 0, 2)


def local(snapshots, outlier_cols, outlier_values, threshold):
    if lax.axis_size("tm") == 8 and lax.axis_size("space") == 4:
        return square(snapshots, outlier_cols, outlier_values, threshold)
    points = snapshots.shape[1] * lax.axis_size("space")
    band = ring(clean(snapshots, outlier_cols, outlier_values, threshold))
    return band * (1.0 / jnp.sqrt(jnp.float32(points)))


def solution(mesh):
    placed = (P("tm", "space"), P("tm", "space"), P("tm", "space", None, None), P())
    return jax.shard_map(
        local, mesh=mesh, in_specs=placed, out_specs=P("tm", None, "space"), check_vma=False
    )
```

```python
import functools
import math

import jax
import jax.numpy as jnp
from jax import lax
from jax.experimental import pallas as pl
from jax.experimental.pallas import tpu as pltpu
from jax.sharding import PartitionSpec as P

ST = 128
SNAP_MAX = 6.0
OUTLIER_MAX = 12.0
UNITS = 4
STAGES = ((0, 1), (2,), (3,))


def swapped(x, axis, bit, only=None):
    pairs = [(i, i ^ bit) for i in range(lax.axis_size(axis)) if only is None or only(i)]
    return lax.ppermute(x, axis, pairs)


def passed_along(x, axis, by):
    size = lax.axis_size(axis)
    return lax.ppermute(x, axis, [(i, (i + by) % size) for i in range(size)])


def tile_product(own, other):
    return lax.dot_general(own, other, (((1,), (1,)), ((), ())), preferred_element_type=jnp.float32)


def clean(snapshots, outlier_cols, outlier_values, threshold):
    block_rows, points = snapshots.shape
    tiles_dev = points // ST
    onehot = (
        outlier_cols[:, :, None] == jnp.arange(tiles_dev, dtype=jnp.int32)[None, None, :]
    ).astype(jnp.bfloat16)
    dense = jnp.einsum("rkos,rkn->rons", outlier_values, onehot, preferred_element_type=jnp.float32)
    dense = dense.reshape(block_rows, points)
    diff = snapshots.astype(jnp.float32) - dense
    return (jnp.sign(diff) * jnp.maximum(jnp.abs(diff) - threshold, 0.0)).astype(jnp.bfloat16)


def ring(cleaned):
    kept = [tile_product(cleaned, cleaned)]
    moving = cleaned
    for step in range(lax.axis_size("tm") // 2):
        moving = passed_along(moving, "tm", -1)
        kept.append(tile_product(cleaned, moving))
    return lax.psum_scatter(jnp.stack(kept, axis=1), "space", scatter_dimension=2, tiled=True)


def on_units(body, out_shape, n_in):
    whole = pl.BlockSpec(memory_space=pltpu.VMEM)
    return pl.pallas_call(
        body,
        out_shape=out_shape,
        in_specs=[whole] * n_in,
        out_specs=jax.tree.map(lambda _: whole, out_shape),
        compiler_params=pltpu.CompilerParams(vmem_limit_bytes=18 << 20),
        cost_estimate=pl.CostEstimate(flops=1000, bytes_accessed=1000, transcendentals=0),
    )


def clean_kernel(
    cols_hbm, threshold_ref, snapshots_hbm, values_hbm, rest_ref, *refs
):
    *sent_refs, cols_ref, snapshots_ref, values_ref, cols_sem, row_sems, value_sems = refs
    tile_rows, listed, height, _ = values_ref.shape
    width = height // UNITS
    threshold = threshold_ref[0]
    cols_copy = pltpu.make_async_copy(cols_hbm, cols_ref, cols_sem)
    cols_copy.start()
    row_copies, value_copies = [], []
    for g in range(tile_rows):
        rows = pl.ds(g * height, height)
        row_copies.append(pltpu.make_async_copy(snapshots_hbm.at[rows], snapshots_ref.at[rows], row_sems.at[g]))
        value_copies.append(pltpu.make_async_copy(values_hbm.at[g], values_ref.at[g], value_sems.at[g]))
        row_copies[-1].start()
        value_copies[-1].start()
    cols_copy.wait()

    def shrunk(d):
        return (d - jnp.clip(d, -threshold, threshold)).astype(jnp.bfloat16)

    for g in range(tile_rows):
        row_copies[g].wait()

        def put(unit, columns, value):
            if unit >= len(STAGES[0]):
                top = (unit - len(STAGES[0])) * height + g * width
                rest_ref[top : top + width, columns] = value
            for stage, sent_ref in enumerate(sent_refs):
                if unit in STAGES[stage]:
                    top = (unit - STAGES[stage][0]) * height + g * width
                    sent_ref[top : top + width, columns] = value

        for unit in range(UNITS):
            rows = slice(g * height + unit * width, g * height + (unit + 1) * width)
            put(unit, slice(None), shrunk(snapshots_ref[rows, :].astype(jnp.float32)))
        value_copies[g].wait()
        for k in range(listed):
            col = cols_ref[g, k]
            columns = pl.ds(pl.multiple_of(col * ST, ST), ST)
            for unit in range(UNITS):
                rows = slice(unit * width, (unit + 1) * width)
                total = values_ref[g, k, rows, :].astype(jnp.float32)
                for other in range(listed):
                    if other != k:
                        same = jnp.where(cols_ref[g, other] == col, 1.0, 0.0)
                        total = total + same * values_ref[g, other, rows, :].astype(jnp.float32)
                rows = slice(g * height + unit * width, g * height + (unit + 1) * width)
                put(unit, columns, shrunk(snapshots_ref[rows, columns].astype(jnp.float32) - total))


def clean_units(snapshots, outlier_cols, outlier_values, threshold):
    rows, points = snapshots.shape
    tile_rows = outlier_values.shape[0]
    length = rows // UNITS
    counts = [UNITS - len(STAGES[0])] + [len(units) for units in STAGES]
    out_shape = [jax.ShapeDtypeStruct((n * length, points), jnp.bfloat16) for n in counts]
    hbm = pl.BlockSpec(memory_space=pltpu.HBM)
    stay_put = functools.partial(pltpu.with_memory_space_constraint, memory_space=pltpu.HBM)
    return pl.pallas_call(
        clean_kernel,
        out_shape=out_shape,
        in_specs=[hbm, pl.BlockSpec(memory_space=pltpu.SMEM), hbm, hbm],
        out_specs=[pl.BlockSpec(memory_space=pltpu.VMEM)] * len(out_shape),
        scratch_shapes=[
            pltpu.SMEM(outlier_cols.shape, jnp.int32),
            pltpu.VMEM(snapshots.shape, jnp.bfloat16),
            pltpu.VMEM(outlier_values.shape, jnp.bfloat16),
            pltpu.SemaphoreType.DMA,
            pltpu.SemaphoreType.DMA((tile_rows,)),
            pltpu.SemaphoreType.DMA((tile_rows,)),
        ],
        compiler_params=pltpu.CompilerParams(vmem_limit_bytes=18 << 20),
    )(stay_put(outlier_cols), threshold.reshape(1), stay_put(snapshots), stay_put(outlier_values))


def columns_of(ref):
    here = lax.axis_index("space")
    width = ref.shape[0] // 4
    return [ref[pl.ds(pl.multiple_of((here ^ q) * width, width), width), :] for q in (0, 2, 1, 3)]


def multiply(cols, rows, stay_ref, away_ref, places):
    cols = [piece for ref in cols for piece in columns_of(ref)]
    product = tile_product(jnp.concatenate(cols, axis=0), jnp.concatenate([ref[...] for ref in rows], axis=0))
    width, length = stay_ref.shape[2:]
    for c, line in enumerate(places):
        for s, place in enumerate(line):
            for q in range(4):
                top = (c * 4 + q) * width
                block = product[top : top + width, s * length : (s + 1) * length]
                (stay_ref, stay_ref, away_ref, away_ref)[q][q % 2, place] = block


def units_of(stage_refs):
    length = stage_refs[0].shape[0] // len(STAGES[0])
    return [ref.at[pl.ds(i * length, length)] for s, ref in enumerate(stage_refs) for i in range(len(STAGES[s]))]


def own_kernel(*refs):
    *own_refs, stay_ref, away_ref = refs
    units = units_of(own_refs)
    for c in range(UNITS):
        multiply([units[c]], units, stay_ref, away_ref, [[c * UNITS + s for s in range(UNITS)]])


def x_blocks(stage):
    fresh, before = STAGES[stage], range(STAGES[stage][0])
    return [(c, s) for c in fresh for s in [*before, *fresh]] + [(c, s) for c in before for s in fresh]


def y_blocks(stage):
    return [(c, s) for c in STAGES[stage] for s in range(UNITS)]


def stage_blocks(stage):
    names = [("near", key) for key in x_blocks(stage)] + [("cross", key) for key in x_blocks(stage)]
    return names + [("y", key) for key in y_blocks(stage)] + [("side", key) for key in y_blocks(stage)]


def stage_kernel(stage, *refs):
    refs = list(refs)

    def take(n):
        out, refs[:n] = refs[:n], []
        return out

    own_refs = take(len(STAGES))
    sibling_refs = take(len(STAGES[0]) if stage == 0 else 1)
    y_ref, y_other_ref = take(2)
    x_refs = take(stage + 1)
    left_before, cross_before = take(stage), take(stage)
    stay_ref, away_ref, left_ref, cross_ref, side_ref = take(5)
    core = lax.rem(lax.axis_index("tm"), 2)
    far = lax.rem(lax.div(lax.axis_index("tm"), 2), 2)
    fresh, before = STAGES[stage], STAGES[stage][0]
    first, count = fresh[0], len(fresh)
    length = own_refs[0].shape[0] // len(STAGES[0])
    sibling_first = (first - len(STAGES[0])) * length if stage > 0 else 0

    def unit_of(ref, i):
        return ref.at[pl.ds(i * length, length)]

    for i in range(count):
        rows = slice(i * length, (i + 1) * length)
        if stage == 0:
            sibling_ref, sibling_rows = sibling_refs[i], slice(None)
        else:
            sibling_ref = sibling_refs[0]
            sibling_rows = slice(sibling_first + i * length, sibling_first + (i + 1) * length)

        @pl.when(far == 1)
        def _():
            left_ref[rows] = y_ref[rows]
            cross_ref[rows] = y_other_ref[rows]

        @pl.when(far == 0)
        def _():
            left_ref[rows] = own_refs[stage][rows]
            cross_ref[rows] = sibling_ref[sibling_rows]

        @pl.when(core == 0)
        def _():
            side_ref[rows] = sibling_ref[sibling_rows]

        @pl.when(core == 1)
        def _():
            side_ref[rows] = y_other_ref[rows]

    place = {key: i for i, key in enumerate(stage_blocks(stage))}
    x_units = units_of(x_refs)
    left, cross = units_of([*left_before, left_ref]), units_of([*cross_before, cross_ref])
    n = first + count
    multiply(
        x_units[first:],
        left + cross,
        stay_ref,
        away_ref,
        [[place[name, (c, s)] for name in ("near", "cross") for s in range(n)] for c in fresh],
    )
    if before > 0:
        multiply(
            x_units[:first],
            left[first:] + cross[first:],
            stay_ref,
            away_ref,
            [[place[name, (c, s)] for name in ("near", "cross") for s in fresh] for c in range(before)],
        )
    multiply(
        [unit_of(ref, i) for ref in (y_ref, side_ref) for i in range(count)],
        units_of(own_refs),
        stay_ref,
        away_ref,
        [[place[name, (c, s)] for s in range(UNITS)] for name in ("y", "side") for c in fresh],
    )


def assemble_kernel(scale, own_ref, *refs):
    *total_refs, handed_ref, crossed_ref, handed_last_ref, crossed_last_ref, out_ref = refs
    core = lax.rem(lax.axis_index("tm"), 2)
    far = lax.rem(lax.div(lax.axis_index("tm"), 2), 2)
    where = {("own", (c, s)): (own_ref, c * UNITS + s) for c in range(UNITS) for s in range(UNITS)}
    for stage, ref in enumerate(total_refs):
        where.update({key: (ref, i) for i, key in enumerate(stage_blocks(stage))})
    for i, key in enumerate(x_blocks(0) + x_blocks(1)):
        where.update({("handed", key): (handed_ref, i), ("crossed", key): (crossed_ref, i)})
    for i, key in enumerate(x_blocks(2)):
        where.update({("handed", key): (handed_last_ref, i), ("crossed", key): (crossed_last_ref, i)})
    width = own_ref.shape[1]
    quarter = width * UNITS

    def put(k, name):
        for s in range(UNITS):
            pieces = [where[name, (c, s)] for c in range(UNITS)]
            tile = jnp.concatenate([ref[i] for ref, i in pieces], axis=0).T * scale
            for g in range(4):
                out_ref[k, g * quarter + s * width : g * quarter + (s + 1) * width, :] = tile[g * width : (g + 1) * width]

    put(0, "own")
    put(4, "y")

    @pl.when(far == 0)
    def _():
        put(2, "near")

    @pl.when(far == 1)
    def _():
        put(2, "handed")

    @pl.when(core == 0)
    def _():
        put(1, "side")
        put(3, "crossed")

    @pl.when(core == 1)
    def _():
        put(1, "crossed")
        put(3, "side")


def square(snapshots, outlier_cols, outlier_values, threshold):
    rows, points = snapshots.shape
    width, length = rows // (4 * UNITS), rows // UNITS
    most = SNAP_MAX + outlier_cols.shape[1] * OUTLIER_MAX
    down = 2.0 ** -max(0, math.ceil(math.log2(2 * points * most * most / 6e4)))
    scale = 1.0 / (math.sqrt(points * lax.axis_size("space")) * down)

    def message(blocks):
        return [jax.ShapeDtypeStruct((2, blocks, width, length), jnp.float32)] * 2

    def units(n):
        return jax.ShapeDtypeStruct((n * length, points), jnp.bfloat16)

    def behind(value, *others):
        return lax.optimization_barrier((value, *others))[0]

    def exchanged(away):
        return swapped((away * down).astype(jnp.float16), "space", 1)

    def half_summed(stay, came):
        return stay * down + came.astype(jnp.float32)

    def summed(kept, after=()):
        came = swapped(kept[1].astype(jnp.float16), "space", 2)
        return kept[0] + behind(came, *after).astype(jnp.float32)

    def handed_over(stages):
        counts = [len(x_blocks(stage)) for stage in stages]
        near = jnp.concatenate([totals[stage][:n] for n, stage in zip(counts, stages)]).astype(jnp.float16)
        cross = jnp.concatenate([totals[stage][n : 2 * n] for n, stage in zip(counts, stages)]).astype(jnp.float16)
        pairs = [(i, i ^ (5 if i & 2 else 1)) for i in range(lax.axis_size("tm"))]
        return [swapped(near, "tm", 4, lambda i: i & 2), lax.ppermute(cross, "tm", pairs)]

    rest, *sent = clean_units(snapshots, outlier_cols, outlier_values, threshold)
    stay, away = on_units(own_kernel, message(UNITS * UNITS), len(sent))(*sent)
    own_came = exchanged(away)
    own = summed(half_summed(stay, own_came))
    sibling = [swapped(sent[0][:length], "tm", 1)]
    sibling.append(swapped(behind(sent[0][length:], own), "tm", 1))
    x_units, by_y, left, cross, halves, totals, came = [], [], [], [], [], [], None
    for stage, fresh in enumerate(STAGES):
        block = sent[stage]
        if stage > 0:
            block = behind(block, x_units[-1], by_y[-1])
        x_units.append(swapped(block, "tm", 2))
        by_y.append(swapped(block, "tm", 4))
        other = swapped(behind(by_y[-1], x_units[-1], *([own_came], left, left[1:])[stage]), "tm", 1)
        if stage == 1:
            sibling = [swapped(behind(rest, left[0]), "tm", 1)]
        if stage == 2:
            totals.append(summed(halves[0], after=left[1:]))
            other = behind(other, came, *totals)
        elif stage == 1:
            other = behind(other, came)
        operands = [*sent, *sibling, by_y[-1], other, *x_units, *left, *cross]
        out_shape = message(len(stage_blocks(stage))) + [units(len(fresh))] * 3
        stay, away, left_now, cross_now, _ = on_units(
            functools.partial(stage_kernel, stage), out_shape, len(operands)
        )(*operands)
        left.append(left_now)
        cross.append(cross_now)
        came = exchanged(away)
        halves.append(half_summed(stay, came))
    totals.append(summed(halves[1], after=[came]))
    parts = handed_over([0, 1])
    totals.append(summed(halves[2], after=parts))
    parts += handed_over([2])

    out_shape = jax.ShapeDtypeStruct((5, rows, rows // 4), jnp.float32)
    operands = [own, *totals, *(part.astype(jnp.float32) for part in parts)]
    band = on_units(functools.partial(assemble_kernel, scale), out_shape, len(operands))(*operands)
    return band.transpose(1, 0, 2)


def local(snapshots, outlier_cols, outlier_values, threshold):
    if lax.axis_size("tm") == 8 and lax.axis_size("space") == 4:
        return square(snapshots, outlier_cols, outlier_values, threshold)
    points = snapshots.shape[1] * lax.axis_size("space")
    band = ring(clean(snapshots, outlier_cols, outlier_values, threshold))
    return band * (1.0 / jnp.sqrt(jnp.float32(points)))


def solution(mesh):
    placed = (P("tm", "space"), P("tm", "space"), P("tm", "space", None, None), P())
    return jax.shard_map(
        local, mesh=mesh, in_specs=placed, out_specs=P("tm", None, "space"), check_vma=False
    )
```
